32 devices in a mesh: groups: 2 (over y), gx: 4 (over z), gy: 4 (over x, core).
Axes of the slice: x: 2, y: 2, z: 4, core: 2. Of those that a mesh axis runs over, the one named last changes fastest.
Arguments:
- hidden_in: bfloat16 [64, 2, 16384], P(('groups', 'gy'), None, 'gx'), parts along dimension 0, may hold values from -6 to 6
- joined_projection_weight: bfloat16 [16384, 14336], P('gx', 'gy'), may hold values from -0.046875 to 0.046875
- w_out: bfloat16 [12288, 16384], P('gy', 'gx'), may hold values from -0.21875 to 0.21875
- key_cache: bfloat16 [64, 768, 8, 128], P(('groups', 'gx'), None, 'gy'), parts along dimension 0, may hold values from -400 to 400
- cached_value_rows: bfloat16 [64, 768, 8, 128], P(('groups', 'gx'), None, 'gy'), parts along dimension 0, may hold values from -6 to 6
- lengths: int32 [64], P(('groups', 'gx')), parts along dimension 0, may hold values from 192 to 768, as said below
- positions: int32 [64], P(('groups', 'gx')), parts along dimension 0, may hold values from 0 to 32767
Outputs:
- output: bfloat16 [64, 2, 16384], P(('groups', 'gy'), None, 'gx'), parts along dimension 0
The draws below stay inside these ranges and needn't reach their ends.
There are 2 independent parts, one for each index of `groups`. The reference program is written for one: setup_inputs(seed, part) draws one part's arguments, and reference() takes and returns one part's arrays. A program takes and returns all parts, laid end to end along the dimension named above; an argument that names none is the same for every part. Nothing has to cross between parts.
Inputs may be any that keep to these rules, and one draw needn't show every extreme that they name: `lengths`: some request's cache is full at 768 slots.
All inputs are finite; a program needn't handle non-finite values.
Results may differ from the reference program's by a relative error of at most 0.011.
Values may be sent and summed in bfloat16 or wider, within the bound.
No kernel may reach another device: no remote copies, remote signals or barrier semaphores. Data moves between devices by JAX's collectives and lax.ppermute only.
A program may use at most 128 MiB of HBM per device.

```python
import math
import jax
import jax.numpy as jnp
from jax import lax

MODEL_WIDTH = 16384
QUERY_HEADS = 96
KEY_VALUE_HEADS = 8
HEAD_SIZE = 128
CACHE_SLOTS = 768
REQUEST_COUNT = 32


def draw_key_cache(key, part):
    key = jax.random.fold_in(key, 11)
    first_key = jax.random.fold_in(key, 0)
    cache_layout_dims = (REQUEST_COUNT, CACHE_SLOTS, KEY_VALUE_HEADS, HEAD_SIZE)
    values = jnp.clip(2.0 * jax.random.normal(first_key, cache_layout_dims, jnp.float32), -12.0, 12.0)
    return values.astype(jnp.bfloat16)


def draw_lengths(key, part):
    key = jax.random.fold_in(key, 12)
    first_key, random_key_second = jax.random.split(key, 2)
    drawn = jax.random.randint(first_key, (REQUEST_COUNT,), CACHE_SLOTS // 4, CACHE_SLOTS + 1, dtype=jnp.int32)
    full_row = jax.random.randint(random_key_second, (), 0, REQUEST_COUNT, dtype=jnp.int32)
    return jnp.where(jnp.arange(REQUEST_COUNT, dtype=jnp.int32) == full_row, CACHE_SLOTS, drawn).astype(jnp.int32)


def touch_ends(values, own_key, least, high):
    longest = values.shape.index(max(values.shape))
    spots = []
    for shift in (0, 1):
        where = [jax.random.randint(jax.random.fold_in(own_key, axis), (), 0, length) for axis, length in enumerate(values.shape)]
        where[longest] = (where[longest] + shift) % values.shape[longest]
        spots.append(tuple(where))
    return values.at[spots[0]].set(least).at[spots[1]].set(high)


def block_scale(rng, shape, cuts, low, largest):
    def one(position, shards_of):
        heights = jax.random.uniform(jax.random.fold_in(jax.random.fold_in(rng, 6), position), (shards_of,), jnp.float32, low / len(cuts), largest / len(cuts))
        return jnp.repeat(jnp.exp(heights), shape[position] // shards_of).reshape((-1,) + (1,) * (len(shape) - position - 1))

    factor_of = one(*cuts[0])
    for cut in cuts[1:]:
        factor_of = factor_of * one(*cut)
    return factor_of


def gaussian(rng, dims, width, reach, cuts=(), kind=jnp.bfloat16):
    values = jax.random.normal(rng, dims, jnp.float32) * width
    if len(cuts) > 0:
        values = block_scale(rng, dims, cuts, -0.22, 0.18) * values
    return jnp.clip(values, min=-reach, max=reach).astype(kind)


def setup_inputs(seed: int = 0, part: int = 0) -> dict:
    key_list = jax.random.split(jax.random.key(seed), 8)
    part_splits = jax.random.split(jax.random.fold_in(key_list[7], part), 8)
    return {
        "hidden_in": gaussian(part_splits[0], (REQUEST_COUNT, 2, MODEL_WIDTH), 1.0, 6.0, ((0, 4), (2, 4))),
        "joined_projection_weight": gaussian(key_list[1], (MODEL_WIDTH, KEY_VALUE_HEADS * (QUERY_HEADS // KEY_VALUE_HEADS + 2) * HEAD_SIZE), MODEL_WIDTH ** -0.5, 0.046875, ((0, 4), (1, 4))),
        "w_out": gaussian(key_list[2], (QUERY_HEADS * HEAD_SIZE, MODEL_WIDTH), (QUERY_HEADS * HEAD_SIZE // 16) ** -0.5, 0.21875, ((0, 4), (1, 4))),
        "key_cache": draw_key_cache(jax.random.fold_in(jax.random.fold_in(key_list[7], part), 71), part),
        "cached_value_rows": gaussian(part_splits[4], (REQUEST_COUNT, CACHE_SLOTS, KEY_VALUE_HEADS, HEAD_SIZE), 1.0, 6.0, ((0, 4), (2, 4))),
        "lengths": draw_lengths(jax.random.fold_in(jax.random.fold_in(key_list[7], part), 71), part),
        "positions": touch_ends(jax.random.randint(part_splits[6], (REQUEST_COUNT,), 0, 32768), jax.random.fold_in(part_splits[6], 1), 0, 32767).astype(jnp.int32),
    }


def angles(positions, head_dim):
    step_pos = positions.astype(jnp.float32)[:, None] + jnp.arange(2, dtype=jnp.float32)[None, :]
    frequencies = jnp.exp(jnp.arange(head_dim // 2, dtype=jnp.float32) * (-2.0 * math.log(500000.0) / head_dim))
    turned = step_pos[:, :, None] * frequencies
    return (jnp.cos(turned), jnp.sin(turned))

def rotate(values, cosine, sine_part):
    half_dim = values.shape[-1] // 2
    first_half = values[..., :half_dim]
    second = values[..., half_dim:]
    return jnp.concatenate([first_half * cosine - second * sine_part, second * cosine + first_half * sine_part], axis=-1)

def attend(joined_rows, key_cache, cached_value_rows, lengths, positions):
    row_count = joined_rows.shape[0]
    kv_groups = key_cache.shape[2]
    head_dim = key_cache.shape[3]
    cache_len = key_cache.shape[1]
    per_group = joined_rows.shape[2] // (kv_groups * head_dim) - 2
    splitted = joined_rows.reshape(row_count, 2, kv_groups, per_group + 2, head_dim)
    cosine, sine_part = angles(positions, head_dim)
    queries = rotate(splitted[:, :, :, :per_group, :], cosine[:, :, None, None, :], sine_part[:, :, None, None, :]).astype(jnp.bfloat16)
    new_key = rotate(splitted[:, :, :, per_group, :], cosine[:, :, None, :], sine_part[:, :, None, :]).astype(jnp.bfloat16)
    new_value = splitted[:, :, :, per_group + 1, :].astype(jnp.bfloat16)
    score_scale = 1.0 / math.sqrt(head_dim)
    hp = lax.Precision.HIGHEST
    cached = jnp.einsum('rtgqe,rcge->rtgqc', queries.astype(jnp.float32), key_cache.astype(jnp.float32), precision=hp) * score_scale
    fresh_scores = jnp.einsum('rtgqe,rsge->rtgqs', queries.astype(jnp.float32), new_key.astype(jnp.float32), precision=hp) * score_scale
    cache_live = jnp.arange(cache_len, dtype=jnp.int32)[None, :] < lengths[:, None]
    fresh_live = jnp.arange(2, dtype=jnp.int32)[None, :] <= jnp.arange(2, dtype=jnp.int32)[:, None]
    cached = jnp.where(cache_live[:, None, None, None, :], cached, -1e+30)
    fresh_scores = jnp.where(fresh_live[None, :, None, None, :], fresh_scores, -1e+30)
    row_max = jnp.maximum(cached.max(axis=-1), fresh_scores.max(axis=-1))[..., None]
    cached_exp = jnp.exp(cached - row_max)
    fresh_exp = jnp.exp(fresh_scores - row_max)
    denom_sum = cached_exp.sum(axis=-1, keepdims=True) + fresh_exp.sum(axis=-1, keepdims=True)
    cached_w = (cached_exp / denom_sum).astype(jnp.bfloat16)
    fresh_w = (fresh_exp / denom_sum).astype(jnp.bfloat16)
    attended = jnp.einsum('rtgqc,rcge->rtgqe', cached_w.astype(jnp.float32), cached_value_rows.astype(jnp.float32), precision=hp)
    attended = attended + jnp.einsum('rtgqs,rsge->rtgqe', fresh_w.astype(jnp.float32), new_value.astype(jnp.float32), precision=hp)
    return attended.astype(jnp.bfloat16).reshape(row_count, 2, kv_groups * per_group * head_dim)

def reference(hidden_in, joined_projection_weight, w_out, key_cache, cached_value_rows, lengths, positions):
    flat_rows = hidden_in.reshape(REQUEST_COUNT * 2, MODEL_WIDTH)
    joined_rows = jnp.dot(flat_rows, joined_projection_weight, preferred_element_type=jnp.float32).reshape(REQUEST_COUNT, 2, -1)
    attended = attend(joined_rows, key_cache, cached_value_rows, lengths, positions)
    output = jnp.dot(attended.reshape(REQUEST_COUNT * 2, -1), w_out, preferred_element_type=jnp.float32)
    return output.reshape(REQUEST_COUNT, 2, MODEL_WIDTH).astype(jnp.bfloat16)
```

```python
import functools
import math

import jax
import jax.numpy as jnp
import numpy as np
from jax import lax
from jax.experimental import pallas as pl
from jax.experimental.pallas import tpu as pltpu
from jax.sharding import PartitionSpec as P

BF16 = jnp.bfloat16
F32 = jnp.float32
IN_VMEM = pl.BlockSpec(memory_space=pltpu.VMEM)
IN_SMEM = pl.BlockSpec(memory_space=pltpu.SMEM)
ANYWHERE = pl.BlockSpec(memory_space=pl.ANY)
HEAD_PAD = 16


def partner(index, step, count):
    if count & (count - 1) == 0:
        return index ^ step
    return lax.rem(index + count - step, count) if not isinstance(index, int) else (index - step) % count


def target(index, step, count):
    if count & (count - 1) == 0:
        return index ^ step
    return lax.rem(index + step, count) if not isinstance(index, int) else (index + step) % count


def swap(block, axis, step, count):
    return lax.ppermute(block, axis, [(i, target(i, step, count)) for i in range(count)])


def hbm(array):
    return pltpu.with_memory_space_constraint(array, pltpu.HBM)


def vmem(array):
    return pltpu.with_memory_space_constraint(array, pltpu.VMEM)


def rows_at(index, count):
    return pl.ds(pl.multiple_of(index * count, count), count)


def tile_of(width):
    for tile in (512, 256, 128):
        if width % tile == 0:
            return tile
    return width


def fetch_kernel(columns, tile, w_ref, o_ref, sems):
    copies = [
        pltpu.make_async_copy(
            w_ref.at[:, pl.ds(i * tile, tile)], o_ref.at[:, pl.ds(i * tile, tile)], sems.at[i]
        )
        for i in range(columns // tile)
    ]
    for copy in copies:
        copy.start()
    for copy in copies:
        copy.wait()


def fetch(weight, columns, tile, name, after=()):
    depth = weight.shape[0]
    count = len(after)

    def kernel(*refs):
        w_ref, rest = refs[0], refs[1 + count :]
        fetch_kernel(columns, tile, w_ref, *rest)

    return pl.pallas_call(
        kernel,
        out_shape=pltpu.VMEM((depth, columns), weight.dtype),
        in_specs=[ANYWHERE] * (1 + count),
        out_specs=IN_VMEM,
        scratch_shapes=[pltpu.SemaphoreType.DMA((columns // tile,))],
        cost_estimate=pl.CostEstimate(
            flops=0, bytes_accessed=2 * depth * columns * 2, transcendentals=0
        ),
        compiler_params=pltpu.CompilerParams(vmem_limit_bytes=1 << 20),
        name=name,
    )(hbm(weight), *after)


def project_kernel(ngx, ngy, tile, ready, *refs):
    x_refs = refs[:ngy]
    wa_ref, w_ref, k_ref, v_ref = refs[ngy : ngy + 4]
    outs = refs[ngy + 4 :]
    own_ref, send_refs = outs[0], outs[1:ngx]
    kv_ref, vv_ref = outs[ngx : ngx + 2]
    xs, acc, wb, sems, cache_sems = outs[ngx + 2 :]
    depth, width = w_ref.shape
    tiles = width // tile
    rest = [
        pltpu.make_async_copy(w_ref.at[:, pl.ds(i * tile, tile)], wb.at[i - ready], sems.at[i - ready])
        for i in range(ready, tiles)
    ]
    for copy in rest:
        copy.start()
    caches = [
        pltpu.make_async_copy(k_ref, kv_ref, cache_sems.at[0]),
        pltpu.make_async_copy(v_ref, vv_ref, cache_sems.at[1]),
    ]
    for copy in caches:
        copy.start()
    me_x, me_y = lax.axis_index("gx"), lax.axis_index("gy")
    block_rows = xs.shape[0] // ngy
    for step in range(ngy):
        xs[rows_at(partner(me_y, step, ngy), block_rows), :] = x_refs[step][...].reshape(block_rows, depth)

    @pl.loop(0, ready)
    def _(i):
        columns = pl.ds(pl.multiple_of(i * tile, tile), tile)
        acc[:, columns] = jnp.dot(xs[...], wa_ref[:, columns], preferred_element_type=F32)

    for i in range(ready, tiles):
        rest[i - ready].wait()
        acc[:, i * tile : (i + 1) * tile] = jnp.dot(xs[...], wb[i - ready], preferred_element_type=F32)
    part = own_ref.shape[0]
    own_ref[...] = acc[rows_at(me_x, part), :]
    for step in range(1, ngx):
        send_refs[step - 1][...] = acc[rows_at(target(me_x, step, ngx), part), :].astype(BF16)
    for copy in caches:
        copy.wait()


def project(blocks, wa, weight, keys, values, ngx, ngy):
    depth, width = weight.shape
    tile = tile_of(width)
    ready = wa.shape[1] // tile
    rows = 2 * blocks[0].shape[0] * ngy
    part = rows // ngx
    return pl.pallas_call(
        functools.partial(project_kernel, ngx, ngy, tile, ready),
        out_shape=[pltpu.VMEM((part, width), F32)]
        + [pltpu.VMEM((part, width), BF16)] * (ngx - 1)
        + [pltpu.VMEM(keys.shape, keys.dtype), pltpu.VMEM(values.shape, values.dtype)],
        in_specs=[IN_VMEM] * (ngy + 1) + [ANYWHERE] * 3,
        out_specs=[IN_VMEM] * (ngx + 2),
        scratch_shapes=[
            pltpu.VMEM((rows, depth), BF16),
            pltpu.VMEM((rows, width), F32),
            pltpu.VMEM((max(width // tile - ready, 1), depth, tile), BF16),
            pltpu.SemaphoreType.DMA((max(width // tile - ready, 1),)),
            pltpu.SemaphoreType.DMA((2,)),
        ],
        cost_estimate=pl.CostEstimate(
            flops=2 * rows * depth * width, bytes_accessed=depth * width * 2, transcendentals=0
        ),
        compiler_params=pltpu.CompilerParams(vmem_limit_bytes=24 << 20),
        name="project",
    )(*blocks, vmem(wa), hbm(weight), hbm(keys), hbm(values))


def attend_kernel(ngx, groups, per_group, *refs):
    own_ref, recv_refs = refs[0], refs[1:ngx]
    k_ref, v_ref, len_ref, cos_ref, sin_ref, out_ref, qs, at = refs[ngx:]
    tokens, head_dim = own_ref.shape[0], k_ref.shape[2]
    requests, slots = k_ref.shape[0], k_ref.shape[1]
    half = head_dim // 2
    per_request = 2 * HEAD_PAD
    scale = 1.0 / math.sqrt(head_dim)
    cosine, sine = cos_ref[...], sin_ref[...]

    def joined(column):
        s = slice(column * head_dim, (column + 1) * head_dim)
        total = own_ref[:, s]
        for ref in recv_refs:
            total = total + ref[:, s].astype(F32)
        return total

    def rotate(x):
        return x * cosine + pltpu.roll(x, half, 1) * sine

    fresh_keys, fresh_values, fresh = [], [], []
    row = lax.broadcasted_iota(jnp.int32, (tokens * HEAD_PAD, tokens), 0) // HEAD_PAD
    col = lax.broadcasted_iota(jnp.int32, (tokens * HEAD_PAD, tokens), 1)
    fresh_live = (row // 2 == col // 2) & (col <= row)
    for g in range(groups):
        base = g * (per_group + 2)
        for h in range(per_group):
            qs[g, pl.ds(h, tokens, stride=HEAD_PAD), :] = rotate(joined(base + h))
        for h in range(per_group, HEAD_PAD):
            qs[g, pl.ds(h, tokens, stride=HEAD_PAD), :] = jnp.zeros((tokens, head_dim), F32)
        fresh_keys.append(rotate(joined(base + per_group)).astype(BF16))
        fresh_values.append(joined(base + per_group + 1).astype(BF16))
        scores = (
            lax.dot_general(
                qs[g].astype(BF16), fresh_keys[g], (((1,), (1,)), ((), ())), preferred_element_type=F32
            )
            * scale
        )
        fresh.append(jnp.where(fresh_live, scores, -1e30))

    slot = lax.broadcasted_iota(jnp.int32, (1, slots), 1)
    for r in range(requests):
        rows = slice(r * per_request, (r + 1) * per_request)
        q = jnp.concatenate([qs[g, rows, :] for g in range(groups)], axis=0).astype(BF16)
        scores = (
            lax.dot_general(q, k_ref[r], (((1,), (1,)), ((), ())), preferred_element_type=F32) * scale
        )
        live = slot < len_ref[r] * groups
        weights, fresh_weights = [], []
        for g in range(groups):
            mine = live & (lax.rem(slot, groups) == g)
            s = jnp.where(mine, scores[g * per_request : (g + 1) * per_request], -1e30)
            f = fresh[g][rows]
            top = jnp.maximum(s.max(axis=1, keepdims=True), f.max(axis=1, keepdims=True))
            e, fe = jnp.exp(s - top), jnp.exp(f - top)
            inverse = 1.0 / (e.sum(axis=1, keepdims=True) + fe.sum(axis=1, keepdims=True))
            weights.append((e * inverse).astype(BF16))
            fresh_weights.append((fe * inverse).astype(BF16))
        total = jnp.dot(jnp.concatenate(weights, axis=0), v_ref[r], preferred_element_type=F32)
        for g in range(groups):
            at[g, rows, :] = total[g * per_request : (g + 1) * per_request] + jnp.dot(
                fresh_weights[g], fresh_values[g], preferred_element_type=F32
            )
    for g in range(groups):
        for h in range(per_group):
            c = (g * per_group + h) * head_dim
            out_ref[:, c : c + head_dim] = at[g, pl.ds(h, tokens, stride=HEAD_PAD), :].astype(BF16)


def attend(own, received, keys, values, lengths, cosine, sine, groups):
    tokens, width = own.shape
    head_dim = keys.shape[2]
    per_group = width // (groups * head_dim) - 2
    ngx = len(received) + 1
    return pl.pallas_call(
        functools.partial(attend_kernel, ngx, groups, per_group),
        out_shape=pltpu.VMEM((tokens, groups * per_group * head_dim), BF16),
        in_specs=[IN_VMEM] * (ngx + 2) + [IN_SMEM] + [IN_VMEM] * 2,
        out_specs=IN_VMEM,
        scratch_shapes=[
            pltpu.VMEM((groups, tokens * HEAD_PAD, head_dim), F32),
            pltpu.VMEM((groups, tokens * HEAD_PAD, head_dim), F32),
        ],
        cost_estimate=pl.CostEstimate(flops=1 << 30, bytes_accessed=8 << 20, transcendentals=1 << 20),
        compiler_params=pltpu.CompilerParams(vmem_limit_bytes=12 << 20),
        name="attend",
    )(own, *received, vmem(keys), vmem(values), lengths, cosine, sine)


def output_kernel(ngx, ngy, tile, *refs):
    a_refs = refs[:ngx]
    w_ref = refs[ngx]
    own_ref, send_refs = refs[ngx + 1], refs[ngx + 2 : ngx + 1 + ngy]
    xs, acc = refs[ngx + 1 + ngy :]
    me_x, me_y = lax.axis_index("gx"), lax.axis_index("gy")
    block_rows = a_refs[0].shape[0]
    for step in range(ngx):
        xs[rows_at(partner(me_x, step, ngx), block_rows), :] = a_refs[step][...]

    @pl.loop(0, w_ref.shape[1] // tile)
    def _(i):
        columns = pl.ds(pl.multiple_of(i * tile, tile), tile)
        acc[:, columns] = jnp.dot(xs[...], w_ref[:, columns], preferred_element_type=F32)

    part = own_ref.shape[0]
    own_ref[...] = acc[rows_at(me_y, part), :]
    for step in range(1, ngy):
        send_refs[step - 1][...] = acc[rows_at(target(me_y, step, ngy), part), :].astype(BF16)


def output(blocks, weight, ngx, ngy):
    depth, width = weight.shape
    rows = blocks[0].shape[0] * ngx
    part = rows // ngy
    return pl.pallas_call(
        functools.partial(output_kernel, ngx, ngy, tile_of(width)),
        out_shape=[pltpu.VMEM((part, width), F32)] + [pltpu.VMEM((part, width), BF16)] * (ngy - 1),
        in_specs=[IN_VMEM] * (ngx + 1),
        out_specs=[IN_VMEM] * ngy,
        scratch_shapes=[pltpu.VMEM((rows, depth), BF16), pltpu.VMEM((rows, width), F32)],
        cost_estimate=pl.CostEstimate(
            flops=2 * rows * depth * width, bytes_accessed=depth * width * 2, transcendentals=0
        ),
        compiler_params=pltpu.CompilerParams(vmem_limit_bytes=8 << 20),
        name="output",
    )(*blocks, vmem(weight))


def finish_kernel(*refs):
    out_ref = refs[-1]
    total = refs[0][...]
    for ref in refs[1:-1]:
        total = total + ref[...].astype(F32)
    out_ref[...] = total.reshape(out_ref.shape).astype(BF16)


def finish(own, received):
    rows, width = own.shape
    return pl.pallas_call(
        finish_kernel,
        out_shape=jax.ShapeDtypeStruct((rows // 2, 2, width), BF16),
        in_specs=[IN_VMEM] * (1 + len(received)),
        out_specs=IN_VMEM,
        compiler_params=pltpu.CompilerParams(vmem_limit_bytes=8 << 20),
        name="finish",
    )(own, *received)


def rotary(positions, head_dim):
    frequencies = np.exp(
        np.arange(head_dim // 2, dtype=np.float32)
        * np.float32(-2.0 * math.log(500000.0) / head_dim)
    ).astype(np.float32)
    step_pos = positions.astype(F32)[:, None] + jnp.arange(2, dtype=F32)[None, :]
    turned = step_pos[:, :, None] * frequencies
    cosine, sine = jnp.cos(turned), jnp.sin(turned)
    rows = 2 * positions.shape[0]
    return (
        jnp.concatenate([cosine, cosine], axis=-1).reshape(rows, head_dim),
        jnp.concatenate([-sine, sine], axis=-1).reshape(rows, head_dim),
    )


def on_device(
    ngx, ngy, hidden_in, joined_projection_weight, w_out, key_cache, cached_value_rows, lengths, positions
):
    requests, cache_len, groups, head_dim = key_cache.shape
    keys = key_cache.reshape(requests, cache_len * groups, head_dim)
    values = cached_value_rows.reshape(requests, cache_len * groups, head_dim)
    cosine, sine = rotary(positions, head_dim)

    blocks = [hidden_in] + [swap(hidden_in, "gy", s, ngy) for s in range(1, ngy)]
    width = joined_projection_weight.shape[1]
    tile = tile_of(width)
    tiles = width // tile
    wa = fetch(joined_projection_weight, max(1, tiles * 4 // 7) * tile, tile, "fetch_joined")
    made = project(blocks, wa, joined_projection_weight, keys, values, ngx, ngy)
    own, sends, keys_near, values_near = made[0], made[1:ngx], made[ngx], made[ngx + 1]

    received = [swap(sends[s - 1], "gx", s, ngx) for s in range(1, ngx)]
    wo = fetch(w_out, w_out.shape[1], tile_of(w_out.shape[1]), "fetch_out", (own,))
    attended = attend(own, received, keys_near, values_near, lengths, cosine, sine, groups)

    parts = [attended] + [swap(attended, "gx", s, ngx) for s in range(1, ngx)]
    made = output(parts, wo, ngx, ngy)
    return finish(made[0], [swap(made[s], "gy", s, ngy) for s in range(1, ngy)])


def solution(mesh):
    in_specs = (
        P(("groups", "gy"), None, "gx"),
        P("gx", "gy"),
        P("gy", "gx"),
        P(("groups", "gx"), None, "gy", None),
        P(("groups", "gx"), None, "gy", None),
        P(("groups", "gx")),
        P(("groups", "gx")),
    )
    out_specs = P(("groups", "gy"), None, "gx")
    return jax.shard_map(
        functools.partial(on_device, mesh.shape["gx"], mesh.shape["gy"]),
        mesh=mesh,
        in_specs=in_specs,
        out_specs=out_specs,
        check_vma=False,
    )
```

```python
import functools
import math

import jax
import jax.numpy as jnp
import numpy as np
from jax import lax
from jax.experimental import pallas as pl
from jax.experimental.pallas import tpu as pltpu
from jax.sharding import PartitionSpec as P

BF16 = jnp.bfloat16
F32 = jnp.float32
IN_VMEM = pl.BlockSpec(memory_space=pltpu.VMEM)
IN_SMEM = pl.BlockSpec(memory_space=pltpu.SMEM)
ANYWHERE = pl.BlockSpec(memory_space=pl.ANY)
HEAD_PAD = 16


def partner(index, step, count):
    if count & (count - 1) == 0:
        return index ^ step
    return lax.rem(index + count - step, count) if not isinstance(index, int) else (index - step) % count


def target(index, step, count):
    if count & (count - 1) == 0:
        return index ^ step
    return lax.rem(index + step, count) if not isinstance(index, int) else (index + step) % count


def swap(block, axis, step, count):
    return lax.ppermute(block, axis, [(i, target(i, step, count)) for i in range(count)])


def hbm(array):
    return pltpu.with_memory_space_constraint(array, pltpu.HBM)


def vmem(array):
    return pltpu.with_memory_space_constraint(array, pltpu.VMEM)


def rows_at(index, count):
    return pl.ds(pl.multiple_of(index * count, count), count)


def dot(x, w):
    return jnp.dot(x, w, preferred_element_type=F32)


def column_tiles(width, tile=512):
    return [slice(c, min(c + tile, width)) for c in range(0, width, tile)]


def columns_in_two_steps(width, body):
    half = width // 2

    if width % 256:
        for s in column_tiles(width):
            body(pl.ds(s.start, s.stop - s.start))
        return

    @pl.loop(0, 2)
    def _(step):
        for s in column_tiles(half):
            body(pl.ds(pl.multiple_of(step * half + s.start, 128), s.stop - s.start))


def cost(flops, read):
    return pl.CostEstimate(flops=flops, bytes_accessed=read, transcendentals=0)


def fetch(weight, width, keys, values, positions, frequencies, groups):
    depth = weight.shape[0]
    requests, rows, head_dim = keys.shape
    slots = rows // groups
    pieces = 4
    piece = depth // pieces

    def kernel(*refs):
        w_ref, k_ref, v_ref, pos_any, freq_any, near_ref, cos_ref, sin_ref = refs[:8]
        split_refs, rest = refs[8 : 8 + 2 * groups], refs[8 + 2 * groups :]
        raw, wide, pos_ref, freq_ref, w_sems, c_sems, s_sems = rest
        small = [
            pltpu.make_async_copy(pos_any, pos_ref, s_sems.at[0]),
            pltpu.make_async_copy(freq_any, freq_ref, s_sems.at[1]),
        ]
        for copy in small:
            copy.start()
        caches = []
        for r in range(requests):
            for n, ref in enumerate((k_ref, v_ref)):
                copy = pltpu.make_async_copy(ref.at[r], raw.at[n, r], c_sems.at[n, r])
                copy.start()
                caches.append((n, r, copy))
        copies = []
        for i in range(pieces):
            s = pl.ds(i * piece, piece)
            copy = pltpu.make_async_copy(w_ref.at[s, pl.ds(0, width)], near_ref.at[s], w_sems.at[i])
            copy.start()
            copies.append(copy)

        for copy in small:
            copy.wait()
        row = lax.broadcasted_iota(jnp.int32, (2 * requests, head_dim), 0)
        place = row % 2
        for r in range(requests):
            place = place + jnp.where(row // 2 == r, pos_ref[r], 0)
        turned = place.astype(F32) * freq_ref[...]
        lane = lax.broadcasted_iota(jnp.int32, (2 * requests, head_dim), 1)
        cos_ref[...] = jnp.cos(turned)
        sine = jnp.sin(turned)
        sin_ref[...] = jnp.where(lane < head_dim // 2, -sine, sine)

        for n, r, copy in caches:
            copy.wait()
            wide[n] = raw[n, r].astype(F32)
            for g in range(groups):
                split_refs[n * groups + g][r] = wide[n, pl.ds(g, slots, stride=groups), :].astype(BF16)
        for copy in copies:
            copy.wait()

    cache = pltpu.VMEM((requests, slots, head_dim), BF16)
    angle = pltpu.VMEM((2 * requests, head_dim), F32)
    return pl.pallas_call(
        kernel,
        out_shape=[pltpu.VMEM((depth, width), weight.dtype), angle, angle] + [cache] * (2 * groups),
        in_specs=[ANYWHERE] * 5,
        out_specs=[IN_VMEM] * (3 + 2 * groups),
        scratch_shapes=[
            pltpu.VMEM((2, requests, rows, head_dim), BF16),
            pltpu.VMEM((2, rows, head_dim), F32),
            pltpu.SMEM((requests,), jnp.int32),
            pltpu.VMEM((1, head_dim), F32),
            pltpu.SemaphoreType.DMA((pieces,)),
            pltpu.SemaphoreType.DMA((2, requests)),
            pltpu.SemaphoreType.DMA((2,)),
        ],
        cost_estimate=cost(0, 4 * depth * width),
        compiler_params=pltpu.CompilerParams(vmem_limit_bytes=12 << 20),
        name="fetch",
    )(hbm(weight), hbm(keys), hbm(values), hbm(positions), hbm(frequencies))


def project(blocks, near, weight, group, groups, width, ahead, ngx, ngy):
    depth, ready = near.shape
    late = width - ready
    count = len(blocks)
    rows = 2 * blocks[0].shape[0] * ngy if count > 1 else blocks[0].shape[0]
    part = rows // ngx
    last = group == groups - 1
    first = group * width
    pieces = 4
    piece = depth // pieces

    def kernel(*refs):
        x_refs, (near_ref, w_ref, own_ref), rest = refs[:count], refs[count : count + 3], refs[count + 3 :]
        send_refs, rest = rest[: ngx - 1], rest[ngx - 1 :]
        if not last:
            next_ref, rest = rest[0], rest[1:]
        if count > 1:
            xs, rest = rest[0], rest[1:]
        else:
            xs = x_refs[0]
        total, sems = rest[:2]

        def copies(begin, wide, to, row):
            made = []
            for i in range(pieces):
                s = pl.ds(i * piece, piece)
                copy = pltpu.make_async_copy(w_ref.at[s, pl.ds(begin, wide)], to.at[s], sems.at[row, i])
                copy.start()
                made.append(copy)
            return made

        late_copies = copies(first + ready, late, rest[2], 0) if late else []
        next_copies = [] if last else copies(first + width, ahead, next_ref, 1)
        me_x, me_y = lax.axis_index("gx"), lax.axis_index("gy")
        if count > 1:
            for step in range(ngy):
                xs[rows_at(partner(me_y, step, ngy), rows // ngy), :] = x_refs[step][...].reshape(
                    rows // ngy, depth
                )
        def product(s):
            total[:, s] = dot(xs[...], near_ref[:, s])

        columns_in_two_steps(ready, product)
        for copy in late_copies:
            copy.wait()
        for s in column_tiles(late):
            total[:, ready + s.start : ready + s.stop] = dot(xs[...], rest[2][:, s])
        own_ref[...] = total[rows_at(me_x, part), :]
        for step in range(1, ngx):
            send_refs[step - 1][...] = total[rows_at(target(me_x, step, ngx), part), :].astype(BF16)
        for copy in next_copies:
            copy.wait()

    out_shape = [pltpu.VMEM((part, width), F32)] + [pltpu.VMEM((part, width), BF16)] * (ngx - 1)
    if not last:
        out_shape.append(pltpu.VMEM((depth, ahead), weight.dtype))
    if count > 1:
        out_shape.append(pltpu.VMEM((rows, depth), BF16))
    scratch = [pltpu.VMEM((rows, width), F32), pltpu.SemaphoreType.DMA((2, pieces))]
    if late:
        scratch.append(pltpu.VMEM((depth, late), weight.dtype))
    return pl.pallas_call(
        kernel,
        out_shape=out_shape,
        in_specs=[IN_VMEM] * (count + 1) + [ANYWHERE],
        out_specs=[IN_VMEM] * len(out_shape),
        scratch_shapes=scratch,
        cost_estimate=cost(2 * rows * depth * width, 2 * depth * width),
        compiler_params=pltpu.CompilerParams(vmem_limit_bytes=14 << 20),
        name="project",
    )(*blocks, vmem(near), hbm(weight))


def attend(own, received, keys, values, lengths, cosine, sine):
    tokens, width = own.shape
    requests, slots, head_dim = keys.shape
    per_group = width // head_dim - 2
    half = head_dim // 2
    rows = 2 * HEAD_PAD
    scale = 1.0 / math.sqrt(head_dim)
    nrecv = len(received)

    def kernel(*refs):
        own_ref, recv_refs = refs[0], refs[1 : 1 + nrecv]
        k_ref, v_ref, len_ref, cos_ref, sin_ref, out_ref, qs, at, sc, wt, fw = refs[1 + nrecv :]
        cosine, sine = cos_ref[...], sin_ref[...]

        def joined(column):
            s = slice(column * head_dim, (column + 1) * head_dim)
            total = own_ref[:, s]
            for ref in recv_refs:
                total = total + ref[:, s].astype(F32)
            return total

        def rotate(x):
            return x * cosine + pltpu.roll(x, half, 1) * sine

        for h in range(HEAD_PAD):
            value = rotate(joined(h)) if h < per_group else jnp.zeros((tokens, head_dim), F32)
            qs[pl.ds(h, tokens, stride=HEAD_PAD), :] = value
        new_key = rotate(joined(per_group)).astype(BF16)
        new_value = joined(per_group + 1).astype(BF16)

        contract = (((1,), (1,)), ((), ()))
        for r in range(requests):
            s = slice(r * rows, (r + 1) * rows)
            sc[s, :] = lax.dot_general(
                qs[s, :].astype(BF16), k_ref[r], contract, preferred_element_type=F32
            )
        fresh = lax.dot_general(qs[...].astype(BF16), new_key, contract, preferred_element_type=F32)
        row = lax.broadcasted_iota(jnp.int32, fresh.shape, 0) // HEAD_PAD
        col = lax.broadcasted_iota(jnp.int32, fresh.shape, 1)
        fresh = jnp.where((row // 2 == col // 2) & (col <= row), fresh * scale, -1e30)

        slot = lax.broadcasted_iota(jnp.int32, (1, slots), 1)
        for r in range(requests):
            s = slice(r * rows, (r + 1) * rows)
            live = slot < len_ref[r]
            score = jnp.where(live, sc[s, :] * scale, -1e30)
            f = fresh[s]
            top = jnp.maximum(score.max(axis=1, keepdims=True), f.max(axis=1, keepdims=True))
            e, fe = jnp.exp(score - top), jnp.exp(f - top)
            inverse = 1.0 / (e.sum(axis=1, keepdims=True) + fe.sum(axis=1, keepdims=True))
            wt[s, :] = (e * inverse).astype(BF16)
            fw[s, :] = (fe * inverse).astype(BF16)
        at[...] = dot(fw[...], new_value)
        for r in range(requests):
            s = slice(r * rows, (r + 1) * rows)
            at[s, :] += dot(wt[s, :], v_ref[r])
        for h in range(per_group):
            out_ref[:, h * head_dim : (h + 1) * head_dim] = at[
                pl.ds(h, tokens, stride=HEAD_PAD), :
            ].astype(BF16)

    return pl.pallas_call(
        kernel,
        out_shape=pltpu.VMEM((tokens, per_group * head_dim), BF16),
        in_specs=[IN_VMEM] * (nrecv + 3) + [IN_SMEM] + [IN_VMEM] * 2,
        out_specs=IN_VMEM,
        scratch_shapes=[
            pltpu.VMEM((tokens * HEAD_PAD, head_dim), F32),
            pltpu.VMEM((tokens * HEAD_PAD, head_dim), F32),
            pltpu.VMEM((requests * rows, slots), F32),
            pltpu.VMEM((requests * rows, slots), BF16),
            pltpu.VMEM((requests * rows, tokens), BF16),
        ],
        cost_estimate=cost(1 << 31, 12 << 20),
        compiler_params=pltpu.CompilerParams(vmem_limit_bytes=10 << 20),
        name="attend",
    )(own, *received, keys, values, lengths, cosine, sine)


def project_out(blocks, acc, weight, first, last, ngx, ngy):
    width = weight.shape[1]
    block_rows, depth = blocks[0].shape
    rows = block_rows * ngx
    part = rows // ngy

    def kernel(*refs):
        a_refs, w_ref, rest = refs[:ngx], refs[ngx], refs[ngx + 1 :]
        if acc is not None:
            acc_ref, rest = rest[0], rest[1:]
        outs, rest = (rest[:ngy], rest[ngy:]) if last else (rest[:1], rest[1:])
        xs = rest[0]
        total = rest[1] if last else outs[0]
        me_x, me_y = lax.axis_index("gx"), lax.axis_index("gy")
        for step in range(ngx):
            xs[rows_at(partner(me_x, step, ngx), block_rows), :] = a_refs[step][...]
        for s in column_tiles(width):
            product = dot(xs[...], w_ref[first : first + depth, s])
            total[:, s] = product if acc is None else acc_ref[:, s] + product
        if last:
            outs[0][...] = total[rows_at(me_y, part), :]
            for step in range(1, ngy):
                outs[step][...] = total[rows_at(target(me_y, step, ngy), part), :].astype(BF16)

    if last:
        out_shape = [pltpu.VMEM((part, width), F32)] + [pltpu.VMEM((part, width), BF16)] * (ngy - 1)
    else:
        out_shape = [pltpu.VMEM((rows, width), F32)]
    extra = [] if acc is None else [acc]
    return pl.pallas_call(
        kernel,
        out_shape=out_shape,
        in_specs=[IN_VMEM] * (ngx + 1 + len(extra)),
        out_specs=[IN_VMEM] * len(out_shape),
        scratch_shapes=[pltpu.VMEM((rows, depth), BF16)]
        + ([pltpu.VMEM((rows, width), F32)] if last else []),
        cost_estimate=cost(2 * rows * depth * width, depth * width * 2),
        compiler_params=pltpu.CompilerParams(vmem_limit_bytes=8 << 20),
        name="project_out",
    )(*blocks, weight, *extra)


def finish(own, received):
    rows, width = own.shape

    def kernel(*refs):
        total = refs[0][...]
        for ref in refs[1:-1]:
            total = total + ref[...].astype(F32)
        refs[-1][...] = total.reshape(rows // 2, 2, width).astype(BF16)

    return pl.pallas_call(
        kernel,
        out_shape=jax.ShapeDtypeStruct((rows // 2, 2, width), BF16),
        in_specs=[IN_VMEM] * (1 + len(received)),
        out_specs=IN_VMEM,
        compiler_params=pltpu.CompilerParams(vmem_limit_bytes=8 << 20),
        name="finish",
    )(own, *received)


def frequencies_of(head_dim):
    half = np.exp(
        np.arange(head_dim // 2, dtype=np.float32)
        * np.float32(-2.0 * math.log(500000.0) / head_dim)
    ).astype(np.float32)
    return jnp.asarray(np.concatenate([half, half])[None])


def on_device(
    ngx, ngy, hidden_in, joined_projection_weight, w_out, key_cache, cached_value_rows, lengths, positions
):
    requests, cache_len, groups, head_dim = key_cache.shape
    keys = key_cache.reshape(requests, cache_len * groups, head_dim)
    values = cached_value_rows.reshape(requests, cache_len * groups, head_dim)
    width = joined_projection_weight.shape[1] // groups
    near_width, ahead = width * 6 // 7 // 256 * 256, width * 4 // 7 // 256 * 256

    rows = [hidden_in] + [swap(hidden_in, "gy", s, ngy) for s in range(1, ngy)]
    near, cosine, sine, *caches = fetch(
        joined_projection_weight, near_width, keys, values, positions, frequencies_of(head_dim), groups
    )
    joined = []
    for g in range(groups):
        made = project(rows, near, joined_projection_weight, g, groups, width, ahead, ngx, ngy)
        joined.append((made[0], [swap(made[s], "gx", s, ngx) for s in range(1, ngx)]))
        if g < groups - 1:
            near = made[ngx]
        if len(rows) > 1:
            rows = [made[-1]]

    attended = []
    for g in range(groups):
        own, received = joined[g]
        mine = attend(own, received, caches[g], caches[groups + g], lengths, cosine, sine)
        attended.append([mine] + [swap(mine, "gx", s, ngx) for s in range(1, ngx)])
    total = None
    depth_out = w_out.shape[0] // groups
    for g in range(groups):
        made = project_out(attended[g], total, w_out, g * depth_out, g == groups - 1, ngx, ngy)
        total = made[0]
    return finish(made[0], [swap(made[s], "gy", s, ngy) for s in range(1, ngy)])


def solution(mesh):
    in_specs = (
        P(("groups", "gy"), None, "gx"),
        P("gx", "gy"),
        P("gy", "gx"),
        P(("groups", "gx"), None, "gy", None),
        P(("groups", "gx"), None, "gy", None),
        P(("groups", "gx")),
        P(("groups", "gx")),
    )
    out_specs = P(("groups", "gy"), None, "gx")
    return jax.shard_map(
        functools.partial(on_device, mesh.shape["gx"], mesh.shape["gy"]),
        mesh=mesh,
        in_specs=in_specs,
        out_specs=out_specs,
        check_vma=False,
    )
```

```python
import functools
import math

import jax
import jax.numpy as jnp
import numpy as np
from jax import lax
from jax.experimental import pallas as pl
from jax.experimental.pallas import tpu as pltpu
from jax.sharding import PartitionSpec as P

BF16 = jnp.bfloat16
F32 = jnp.float32
IN_VMEM = pl.BlockSpec(memory_space=pltpu.VMEM)
IN_SMEM = pl.BlockSpec(memory_space=pltpu.SMEM)
ANYWHERE = pl.BlockSpec(memory_space=pl.ANY)
PIECES = 4


def partner(index, step, count):
    if count & (count - 1) == 0:
        return index ^ step
    return lax.rem(index + count - step, count) if not isinstance(index, int) else (index - step) % count


def target(index, step, count):
    if count & (count - 1) == 0:
        return index ^ step
    return lax.rem(index + step, count) if not isinstance(index, int) else (index + step) % count


def swap(block, axis, step, count):
    return lax.ppermute(block, axis, [(i, target(i, step, count)) for i in range(count)])


def hbm(array):
    return pltpu.with_memory_space_constraint(array, pltpu.HBM)


def vmem(array):
    return pltpu.with_memory_space_constraint(array, pltpu.VMEM)


def rows_at(index, count):
    return pl.ds(pl.multiple_of(index * count, count), count)


def dot(x, w):
    return jnp.dot(x, w, preferred_element_type=F32)


def column_tiles(width, tile=512):
    return [slice(c, min(c + tile, width)) for c in range(0, width, tile)]


def columns_in_two_steps(width, body):
    half = width // 2

    if width % 256:
        for s in column_tiles(width):
            body(pl.ds(s.start, s.stop - s.start))
        return

    @pl.loop(0, 2)
    def _(step):
        for s in column_tiles(half):
            body(pl.ds(pl.multiple_of(step * half + s.start, 128), s.stop - s.start))


def cost(flops, read):
    return pl.CostEstimate(flops=flops, bytes_accessed=read, transcendentals=0)


def chunks_of(groups, per_group, small=8):
    if per_group <= small:
        return [[(g, 0, per_group)] for g in range(groups)]
    first = [(g, 0, per_group) for g in range(groups - 1)] + [(groups - 1, 0, per_group - small)]
    return [first, [(groups - 1, per_group - small, small)]]


def ranges_of(chunk, per_group, unit):
    made = []
    for g, first, count in chunk:
        base = g * (per_group + 2)
        made.append([base + first, count])
        if first == 0:
            made.append([base + per_group, 2])
    merged = []
    for first, count in made:
        if merged and merged[-1][0] + merged[-1][1] == first:
            merged[-1][1] += count
        else:
            merged.append([first, count])
    return [(first * unit, count * unit) for first, count in merged]


def cut(ranges, begin, end):
    made, at = [], 0
    for first, width in ranges:
        low, high = max(begin, at), min(end, at + width)
        if low < high:
            made.append((first + low - at, low - begin, high - low))
        at += width
    return made


def copy_columns(w_ref, to, parts, sems):
    piece = w_ref.shape[0] // PIECES
    made = []
    for n, (source, place, width) in enumerate(parts):
        for i in range(PIECES):
            rows = pl.ds(i * piece, piece)
            copy = pltpu.make_async_copy(
                w_ref.at[rows, pl.ds(source, width)], to.at[rows, pl.ds(place, width)], sems.at[n, i]
            )
            copy.start()
            made.append(copy)
    return made


def fetch(weight, parts, positions, frequencies):
    depth = weight.shape[0]
    width = sum(part[2] for part in parts)
    requests, head_dim = positions.shape[0], frequencies.shape[1]

    def kernel(w_ref, pos_any, freq_any, near_ref, cos_ref, sin_ref, pos_ref, freq_ref, w_sems, s_sems):
        small = [
            pltpu.make_async_copy(pos_any, pos_ref, s_sems.at[0]),
            pltpu.make_async_copy(freq_any, freq_ref, s_sems.at[1]),
        ]
        for copy in small:
            copy.start()
        copies = copy_columns(w_ref, near_ref, parts, w_sems)
        for copy in small:
            copy.wait()
        row = lax.broadcasted_iota(jnp.int32, (2 * requests, head_dim), 0)
        place = row % 2
        for r in range(requests):
            place = place + jnp.where(row // 2 == r, pos_ref[r], 0)
        turned = place.astype(F32) * freq_ref[...]
        lane = lax.broadcasted_iota(jnp.int32, (2 * requests, head_dim), 1)
        cos_ref[...] = jnp.cos(turned)
        sine = jnp.sin(turned)
        sin_ref[...] = jnp.where(lane < head_dim // 2, -sine, sine)
        for copy in copies:
            copy.wait()

    angle = pltpu.VMEM((2 * requests, head_dim), F32)
    return pl.pallas_call(
        kernel,
        out_shape=[pltpu.VMEM((depth, width), weight.dtype), angle, angle],
        in_specs=[ANYWHERE] * 3,
        out_specs=[IN_VMEM] * 3,
        scratch_shapes=[
            pltpu.SMEM((requests,), jnp.int32),
            pltpu.VMEM((1, head_dim), F32),
            pltpu.SemaphoreType.DMA((len(parts), PIECES)),
            pltpu.SemaphoreType.DMA((2,)),
        ],
        cost_estimate=cost(0, 4 * depth * width),
        compiler_params=pltpu.CompilerParams(vmem_limit_bytes=4 << 20),
        name="fetch",
    )(hbm(weight), hbm(positions), hbm(frequencies))


def project(blocks, near, weight, ranges, coming, ngx, ngy):
    depth, ready = near.shape
    width = sum(count for _, count in ranges)
    late_tiles = column_tiles(width - ready, 256)
    late_parts = [cut(ranges, ready + t.start, ready + t.stop) for t in late_tiles]
    ahead = sum(part[2] for part in coming)
    count = len(blocks)
    rows = 2 * blocks[0].shape[0] * ngy if count > 1 else blocks[0].shape[0]
    part = rows // ngx

    def kernel(*refs):
        x_refs, (near_ref, w_ref, own_ref), rest = refs[:count], refs[count : count + 3], refs[count + 3 :]
        send_refs, rest = rest[: ngx - 1], rest[ngx - 1 :]
        if ahead:
            next_ref, rest = rest[0], rest[1:]
        if count > 1:
            xs, rest = rest[0], rest[1:]
        else:
            xs = x_refs[0]
        total, rest = rest[0], rest[1:]
        late_copies = []
        if late_tiles:
            late, late_sems, rest = rest[0], rest[1], rest[2:]
            late_copies = [
                copy_columns(w_ref, late.at[:, pl.ds(t.start, t.stop - t.start)], parts, late_sems.at[i])
                for i, (t, parts) in enumerate(zip(late_tiles, late_parts))
            ]
        next_copies = copy_columns(w_ref, next_ref, coming, rest[0]) if ahead else []
        me_x, me_y = lax.axis_index("gx"), lax.axis_index("gy")
        if count > 1:
            for step in range(ngy):
                xs[rows_at(partner(me_y, step, ngy), rows // ngy), :] = x_refs[step][...].reshape(
                    rows // ngy, depth
                )

        def product(s):
            total[:, s] = dot(xs[...], near_ref[:, s])

        columns_in_two_steps(ready, product)
        for s, arriving in zip(late_tiles, late_copies):
            for copy in arriving:
                copy.wait()
            total[:, ready + s.start : ready + s.stop] = dot(xs[...], late[:, s])
        own_ref[...] = total[rows_at(me_x, part), :]
        for step in range(1, ngx):
            send_refs[step - 1][...] = total[rows_at(target(me_x, step, ngx), part), :].astype(BF16)
        for copy in next_copies:
            copy.wait()

    out_shape = [pltpu.VMEM((part, width), F32)] + [pltpu.VMEM((part, width), BF16)] * (ngx - 1)
    if ahead:
        out_shape.append(pltpu.VMEM((depth, ahead), weight.dtype))
    if count > 1:
        out_shape.append(pltpu.VMEM((rows, depth), BF16))
    scratch = [pltpu.VMEM((rows, width), F32)]
    if late_tiles:
        scratch.append(pltpu.VMEM((depth, width - ready), weight.dtype))
        most = max(len(parts) for parts in late_parts)
        scratch.append(pltpu.SemaphoreType.DMA((len(late_tiles), most, PIECES)))
    if ahead:
        scratch.append(pltpu.SemaphoreType.DMA((len(coming), PIECES)))
    return pl.pallas_call(
        kernel,
        out_shape=out_shape,
        in_specs=[IN_VMEM] * (count + 1) + [ANYWHERE],
        out_specs=[IN_VMEM] * len(out_shape),
        scratch_shapes=scratch,
        cost_estimate=cost(2 * rows * depth * width, 2 * depth * width),
        compiler_params=pltpu.CompilerParams(vmem_limit_bytes=14 << 20),
        name="project",
    )(*blocks, vmem(near), hbm(weight))


def attend(own, received, fresh_pairs, keys, values, lengths, cosine, sine, chunk, keep, groups):
    tokens = own.shape[0]
    requests, slots, head_dim = keys.shape
    half = head_dim // 2
    scale = 1.0 / math.sqrt(head_dim)
    nrecv, npair = len(received), len(fresh_pairs)
    pads = [-(-count // 8) * 8 for _, _, count in chunk]
    starts = [2 * sum(pads[:i]) for i in range(len(pads) + 1)]
    rows, parts = starts[-1], len(chunk)

    def kernel(*refs):
        own_ref, recv_refs, rest = refs[0], refs[1 : 1 + nrecv], refs[1 + nrecv :]
        pair_refs, rest = rest[:npair], rest[npair:]
        k_ref, v_ref, len_ref, cos_ref, sin_ref, out_ref = rest[:6]
        kept_refs, rest = (rest[6:8], rest[8:]) if keep else ((), rest[6:])
        sc, wt = rest[:2]
        qs, at, fw = rest[2 : 2 + parts], rest[2 + parts : 2 + 2 * parts], rest[2 + 2 * parts :]
        cosine, sine = cos_ref[...], sin_ref[...]

        def joined(column):
            s = slice(column * head_dim, (column + 1) * head_dim)
            total = own_ref[:, s]
            for ref in recv_refs:
                total = total + ref[:, s].astype(F32)
            return total

        def rotate(x):
            return x * cosine + pltpu.roll(x, half, 1) * sine

        contract = (((1,), (1,)), ((), ()))
        column, fresh, new_values = 0, [], []
        for n, (_, first, count) in enumerate(chunk):
            pad = pads[n]
            for h in range(pad):
                value = rotate(joined(column + h)) if h < count else jnp.zeros((tokens, head_dim), F32)
                qs[n][pl.ds(h, tokens, stride=pad), :] = value
            column += count
            if first == 0:
                new_key = rotate(joined(column)).astype(BF16)
                new_value = joined(column + 1).astype(BF16)
                column += 2
            else:
                new_key, new_value = pair_refs[0][...], pair_refs[1][...]
            new_values.append(new_value)
            scores = lax.dot_general(
                qs[n][...].astype(BF16), new_key, contract, preferred_element_type=F32
            )
            row = lax.broadcasted_iota(jnp.int32, scores.shape, 0) // pad
            col = lax.broadcasted_iota(jnp.int32, scores.shape, 1)
            fresh.append(jnp.where((row // 2 == col // 2) & (col <= row), scores * scale, -1e30))
        if keep:
            kept_refs[0][...], kept_refs[1][...] = new_key, new_value

        for r in range(requests):
            q = [qs[n][2 * r * pads[n] : 2 * (r + 1) * pads[n], :].astype(BF16) for n in range(parts)]
            sc[r * rows : (r + 1) * rows, :] = lax.dot_general(
                jnp.concatenate(q, axis=0), k_ref[r], contract, preferred_element_type=F32
            )
        slot = lax.broadcasted_iota(jnp.int32, (1, slots), 1)
        mine = [lax.rem(slot, groups) == g for g, _, _ in chunk]
        for r in range(requests):
            live = slot < len_ref[r] * groups
            for n in range(parts):
                s = slice(r * rows + starts[n], r * rows + starts[n + 1])
                own_rows = slice(2 * r * pads[n], 2 * (r + 1) * pads[n])
                score = jnp.where(live & mine[n], sc[s, :] * scale, -1e30)
                f = fresh[n][own_rows]
                top = jnp.maximum(score.max(axis=1, keepdims=True), f.max(axis=1, keepdims=True))
                e, fe = jnp.exp(score - top), jnp.exp(f - top)
                inverse = 1.0 / (e.sum(axis=1, keepdims=True) + fe.sum(axis=1, keepdims=True))
                wt[s, :] = (e * inverse).astype(BF16)
                fw[n][own_rows, :] = (fe * inverse).astype(BF16)
        for n in range(parts):
            at[n][...] = dot(fw[n][...], new_values[n])
        for r in range(requests):
            total = dot(wt[r * rows : (r + 1) * rows, :], v_ref[r])
            for n in range(parts):
                at[n][2 * r * pads[n] : 2 * (r + 1) * pads[n], :] += total[starts[n] : starts[n + 1]]
        column = 0
        for n, (_, _, count) in enumerate(chunk):
            for h in range(count):
                out_ref[:, column : column + head_dim] = at[n][
                    pl.ds(h, tokens, stride=pads[n]), :
                ].astype(BF16)
                column += head_dim

    heads = sum(count for _, _, count in chunk)
    out_shape = [pltpu.VMEM((tokens, heads * head_dim), BF16)]
    if keep:
        out_shape += [pltpu.VMEM((tokens, head_dim), BF16)] * 2
    per_part = [pltpu.VMEM((tokens * pad, head_dim), F32) for pad in pads]
    return pl.pallas_call(
        kernel,
        out_shape=out_shape,
        in_specs=[IN_VMEM] * (1 + nrecv + npair + 2) + [IN_SMEM] + [IN_VMEM] * 2,
        out_specs=[IN_VMEM] * len(out_shape),
        scratch_shapes=[
            pltpu.VMEM((requests * rows, slots), F32),
            pltpu.VMEM((requests * rows, slots), BF16),
        ]
        + per_part
        + per_part
        + [pltpu.VMEM((tokens * pad, tokens), BF16) for pad in pads],
        cost_estimate=cost(1 << 31, 12 << 20),
        compiler_params=pltpu.CompilerParams(vmem_limit_bytes=10 << 20),
        name="attend",
    )(own, *received, *fresh_pairs, keys, values, lengths, cosine, sine)


def project_out(blocks, acc, weight, first, last, ngx, ngy):
    width = weight.shape[1]
    block_rows, depth = blocks[0].shape
    rows = block_rows * ngx
    part = rows // ngy

    def kernel(*refs):
        a_refs, w_ref, rest = refs[:ngx], refs[ngx], refs[ngx + 1 :]
        if acc is not None:
            acc_ref, rest = rest[0], rest[1:]
        outs, rest = (rest[:ngy], rest[ngy:]) if last else (rest[:1], rest[1:])
        xs = rest[0]
        total = rest[1] if last else outs[0]
        me_x, me_y = lax.axis_index("gx"), lax.axis_index("gy")
        for step in range(ngx):
            xs[rows_at(partner(me_x, step, ngx), block_rows), :] = a_refs[step][...]
        for s in column_tiles(width):
            product = dot(xs[...], w_ref[first : first + depth, s])
            total[:, s] = product if acc is None else acc_ref[:, s] + product
        if last:
            outs[0][...] = total[rows_at(me_y, part), :]
            for step in range(1, ngy):
                outs[step][...] = total[rows_at(target(me_y, step, ngy), part), :].astype(BF16)

    if last:
        out_shape = [pltpu.VMEM((part, width), F32)] + [pltpu.VMEM((part, width), BF16)] * (ngy - 1)
    else:
        out_shape = [pltpu.VMEM((rows, width), F32)]
    extra = [] if acc is None else [acc]
    return pl.pallas_call(
        kernel,
        out_shape=out_shape,
        in_specs=[IN_VMEM] * (ngx + 1 + len(extra)),
        out_specs=[IN_VMEM] * len(out_shape),
        scratch_shapes=[pltpu.VMEM((rows, depth), BF16)]
        + ([pltpu.VMEM((rows, width), F32)] if last else []),
        cost_estimate=cost(2 * rows * depth * width, depth * width * 2),
        compiler_params=pltpu.CompilerParams(vmem_limit_bytes=8 << 20),
        name="project_out",
    )(*blocks, weight, *extra)


def finish(own, received):
    rows, width = own.shape

    def kernel(*refs):
        total = refs[0][...]
        for ref in refs[1:-1]:
            total = total + ref[...].astype(F32)
        refs[-1][...] = total.reshape(rows // 2, 2, width).astype(BF16)

    return pl.pallas_call(
        kernel,
        out_shape=jax.ShapeDtypeStruct((rows // 2, 2, width), BF16),
        in_specs=[IN_VMEM] * (1 + len(received)),
        out_specs=IN_VMEM,
        compiler_params=pltpu.CompilerParams(vmem_limit_bytes=8 << 20),
        name="finish",
    )(own, *received)


def frequencies_of(head_dim):
    half = np.exp(
        np.arange(head_dim // 2, dtype=np.float32)
        * np.float32(-2.0 * math.log(500000.0) / head_dim)
    ).astype(np.float32)
    return jnp.asarray(np.concatenate([half, half])[None])


def on_device(
    ngx, ngy, hidden_in, joined_projection_weight, w_out, key_cache, cached_value_rows, lengths, positions
):
    requests, cache_len, groups, head_dim = key_cache.shape
    keys = key_cache.reshape(requests, cache_len * groups, head_dim)
    values = cached_value_rows.reshape(requests, cache_len * groups, head_dim)
    per_group = joined_projection_weight.shape[1] // (groups * head_dim) - 2
    chunks = chunks_of(groups, per_group)
    ranges = [ranges_of(chunk, per_group, head_dim) for chunk in chunks]
    widths = [sum(width for _, width in r) for r in ranges]

    rows = [hidden_in] + [swap(hidden_in, "gy", s, ngy) for s in range(1, ngy)]
    near, cosine, sine = fetch(
        joined_projection_weight,
        cut(ranges[0], 0, max(head_dim, widths[0] * 4 // 5 // 256 * 256)),
        positions,
        frequencies_of(head_dim),
    )
    joined = []
    for n in range(len(chunks)):
        last = n == len(chunks) - 1
        coming = [] if last else cut(ranges[n + 1], 0, max(head_dim, widths[n + 1] * 3 // 4 // 256 * 256))
        made = project(rows, near, joined_projection_weight, ranges[n], coming, ngx, ngy)
        joined.append((made[0], [swap(made[s], "gx", s, ngx) for s in range(1, ngx)]))
        if not last:
            near = made[ngx]
        if len(rows) > 1:
            rows = [made[-1]]

    attended, pair = [], []
    for n, chunk in enumerate(chunks):
        own, received = joined[n]
        keep = n + 1 < len(chunks) and chunks[n + 1][0][1] > 0
        mine, *pair = attend(
            own, received, pair, keys, values, lengths, cosine, sine, chunk, keep, groups
        )
        attended.append([mine] + [swap(mine, "gx", s, ngx) for s in range(1, ngx)])
    total, first = None, 0
    for n in range(len(chunks)):
        made = project_out(attended[n], total, w_out, first, n == len(chunks) - 1, ngx, ngy)
        first += attended[n][0].shape[1]
        total = made[0]
    return finish(made[0], [swap(made[s], "gy", s, ngy) for s in range(1, ngy)])


def solution(mesh):
    in_specs = (
        P(("groups", "gy"), None, "gx"),
        P("gx", "gy"),
        P("gy", "gx"),
        P(("groups", "gx"), None, "gy", None),
        P(("groups", "gx"), None, "gy", None),
        P(("groups", "gx")),
        P(("groups", "gx")),
    )
    out_specs = P(("groups", "gy"), None, "gx")
    return jax.shard_map(
        functools.partial(on_device, mesh.shape["gx"], mesh.shape["gy"]),
        mesh=mesh,
        in_specs=in_specs,
        out_specs=out_specs,
        check_vma=False,
    )
```

```python
import functools
import math

import jax
import jax.numpy as jnp
import numpy as np
from jax import lax
from jax.experimental import pallas as pl
from jax.experimental.pallas import tpu as pltpu
from jax.sharding import PartitionSpec as P

BF16 = jnp.bfloat16
F32 = jnp.float32
IN_VMEM = pl.BlockSpec(memory_space=pltpu.VMEM)
IN_SMEM = pl.BlockSpec(memory_space=pltpu.SMEM)
ANYWHERE = pl.BlockSpec(memory_space=pl.ANY)
PIECES = 4


def partner(index, step, count):
    if count & (count - 1) == 0:
        return index ^ step
    return lax.rem(index + count - step, count) if not isinstance(index, int) else (index - step) % count


def target(index, step, count):
    if count & (count - 1) == 0:
        return index ^ step
    return lax.rem(index + step, count) if not isinstance(index, int) else (index + step) % count


def swap(block, axis, step, count):
    return lax.ppermute(block, axis, [(i, target(i, step, count)) for i in range(count)])


def hbm(array):
    return pltpu.with_memory_space_constraint(array, pltpu.HBM)


def vmem(array):
    return pltpu.with_memory_space_constraint(array, pltpu.VMEM)


def rows_at(index, count):
    return pl.ds(pl.multiple_of(index * count, count), count)


def dot(x, w):
    return jnp.dot(x, w, preferred_element_type=F32)


def column_tiles(width, tile=512):
    return [slice(c, min(c + tile, width)) for c in range(0, width, tile)]


def columns_in_two_steps(width, body):
    half = width // 2

    if width % 256:
        for s in column_tiles(width):
            body(pl.ds(s.start, s.stop - s.start))
        return

    @pl.loop(0, 2)
    def _(step):
        for s in column_tiles(half):
            body(pl.ds(pl.multiple_of(step * half + s.start, 128), s.stop - s.start))


def cost(flops, read):
    return pl.CostEstimate(flops=flops, bytes_accessed=read, transcendentals=0)


def chunks_of(groups, per_group, small=8):
    if per_group <= small:
        return [[(g, 0, per_group)] for g in range(groups)]
    first = [(g, 0, per_group) for g in range(groups - 1)] + [(groups - 1, 0, per_group - small)]
    return [first, [(groups - 1, per_group - small, small)]]


def ranges_of(chunk, per_group, unit):
    made = []
    for g, first, count in chunk:
        base = g * (per_group + 2)
        made.append([base + first, count])
        if first == 0:
            made.append([base + per_group, 2])
    merged = []
    for first, count in made:
        if merged and merged[-1][0] + merged[-1][1] == first:
            merged[-1][1] += count
        else:
            merged.append([first, count])
    return [(first * unit, count * unit) for first, count in merged]


def cut(ranges, begin, end):
    made, at = [], 0
    for first, width in ranges:
        low, high = max(begin, at), min(end, at + width)
        if low < high:
            made.append((first + low - at, low - begin, high - low))
        at += width
    return made


def copy_columns(w_ref, to, parts, sems):
    piece = w_ref.shape[0] // PIECES
    made = []
    for n, (source, place, width) in enumerate(parts):
        for i in range(PIECES):
            rows = pl.ds(i * piece, piece)
            copy = pltpu.make_async_copy(
                w_ref.at[rows, pl.ds(source, width)], to.at[rows, pl.ds(place, width)], sems.at[n, i]
            )
            copy.start()
            made.append(copy)
    return made


def fetch(weight, parts, positions, frequencies):
    depth = weight.shape[0]
    width = sum(part[2] for part in parts)
    requests, head_dim = positions.shape[0], frequencies.shape[1]

    def kernel(w_ref, pos_any, freq_any, near_ref, cos_ref, sin_ref, pos_ref, freq_ref, w_sems, s_sems):
        small = [
            pltpu.make_async_copy(pos_any, pos_ref, s_sems.at[0]),
            pltpu.make_async_copy(freq_any, freq_ref, s_sems.at[1]),
        ]
        for copy in small:
            copy.start()
        copies = copy_columns(w_ref, near_ref, parts, w_sems)
        for copy in small:
            copy.wait()
        row = lax.broadcasted_iota(jnp.int32, (2 * requests, head_dim), 0)
        place = row % 2
        for r in range(requests):
            place = place + jnp.where(row // 2 == r, pos_ref[r], 0)
        turned = place.astype(F32) * freq_ref[...]
        lane = lax.broadcasted_iota(jnp.int32, (2 * requests, head_dim), 1)
        cos_ref[...] = jnp.cos(turned)
        sine = jnp.sin(turned)
        sin_ref[...] = jnp.where(lane < head_dim // 2, -sine, sine)
        for copy in copies:
            copy.wait()

    angle = pltpu.VMEM((2 * requests, head_dim), F32)
    return pl.pallas_call(
        kernel,
        out_shape=[pltpu.VMEM((depth, width), weight.dtype), angle, angle],
        in_specs=[ANYWHERE] * 3,
        out_specs=[IN_VMEM] * 3,
        scratch_shapes=[
            pltpu.SMEM((requests,), jnp.int32),
            pltpu.VMEM((1, head_dim), F32),
            pltpu.SemaphoreType.DMA((len(parts), PIECES)),
            pltpu.SemaphoreType.DMA((2,)),
        ],
        cost_estimate=cost(0, 4 * depth * width),
        compiler_params=pltpu.CompilerParams(vmem_limit_bytes=4 << 20),
        name="fetch",
    )(hbm(weight), hbm(positions), hbm(frequencies))


def project(blocks, near, weight, ranges, coming, ngx, ngy):
    depth, ready = near.shape
    width = sum(count for _, count in ranges)
    late_tiles = column_tiles(width - ready, 256)
    late_parts = [cut(ranges, ready + t.start, ready + t.stop) for t in late_tiles]
    ahead = sum(part[2] for part in coming)
    count = len(blocks)
    rows = 2 * blocks[0].shape[0] * ngy if count > 1 else blocks[0].shape[0]
    part = rows // ngx

    def kernel(*refs):
        x_refs, (near_ref, w_ref, own_ref), rest = refs[:count], refs[count : count + 3], refs[count + 3 :]
        send_refs, rest = rest[: ngx - 1], rest[ngx - 1 :]
        if ahead:
            next_ref, rest = rest[0], rest[1:]
        if count > 1:
            xs, rest = rest[0], rest[1:]
        else:
            xs = x_refs[0]
        total, rest = rest[0], rest[1:]
        late_copies = []
        if late_tiles:
            late, late_sems, rest = rest[0], rest[1], rest[2:]
            late_copies = [
                copy_columns(w_ref, late.at[:, pl.ds(t.start, t.stop - t.start)], parts, late_sems.at[i])
                for i, (t, parts) in enumerate(zip(late_tiles, late_parts))
            ]
        next_copies = copy_columns(w_ref, next_ref, coming, rest[0]) if ahead else []
        me_x, me_y = lax.axis_index("gx"), lax.axis_index("gy")
        if count > 1:
            for step in range(ngy):
                xs[rows_at(partner(me_y, step, ngy), rows // ngy), :] = x_refs[step][...].reshape(
                    rows // ngy, depth
                )

        def product(s):
            total[:, s] = dot(xs[...], near_ref[:, s])

        columns_in_two_steps(ready, product)
        for s, arriving in zip(late_tiles, late_copies):
            for copy in arriving:
                copy.wait()
            total[:, ready + s.start : ready + s.stop] = dot(xs[...], late[:, s])
        own_ref[...] = total[rows_at(me_x, part), :]
        for step in range(1, ngx):
            send_refs[step - 1][...] = total[rows_at(target(me_x, step, ngx), part), :].astype(BF16)
        for copy in next_copies:
            copy.wait()

    out_shape = [pltpu.VMEM((part, width), F32)] + [pltpu.VMEM((part, width), BF16)] * (ngx - 1)
    if ahead:
        out_shape.append(pltpu.VMEM((depth, ahead), weight.dtype))
    if count > 1:
        out_shape.append(pltpu.VMEM((rows, depth), BF16))
    scratch = [pltpu.VMEM((rows, width), F32)]
    if late_tiles:
        scratch.append(pltpu.VMEM((depth, width - ready), weight.dtype))
        most = max(len(parts) for parts in late_parts)
        scratch.append(pltpu.SemaphoreType.DMA((len(late_tiles), most, PIECES)))
    if ahead:
        scratch.append(pltpu.SemaphoreType.DMA((len(coming), PIECES)))
    return pl.pallas_call(
        kernel,
        out_shape=out_shape,
        in_specs=[IN_VMEM] * (count + 1) + [ANYWHERE],
        out_specs=[IN_VMEM] * len(out_shape),
        scratch_shapes=scratch,
        cost_estimate=cost(2 * rows * depth * width, 2 * depth * width),
        compiler_params=pltpu.CompilerParams(vmem_limit_bytes=14 << 20),
        name="project",
    )(*blocks, vmem(near), hbm(weight))


def attend(own, received, fresh_pairs, keys, values, lengths, cosine, sine, chunk, keep, groups):
    tokens = own.shape[0]
    requests, slots, head_dim = keys.shape
    half = head_dim // 2
    scale = 1.0 / math.sqrt(head_dim)
    nrecv, npair = len(received), len(fresh_pairs)
    pads = [-(-count // 8) * 8 for _, _, count in chunk]
    starts = [2 * sum(pads[:i]) for i in range(len(pads) + 1)]
    rows, parts = starts[-1], len(chunk)

    def kernel(*refs):
        own_ref, recv_refs, rest = refs[0], refs[1 : 1 + nrecv], refs[1 + nrecv :]
        pair_refs, rest = rest[:npair], rest[npair:]
        k_ref, v_ref, len_ref, cos_ref, sin_ref, out_ref = rest[:6]
        kept_refs, rest = (rest[6:8], rest[8:]) if keep else ((), rest[6:])
        sc, wt = rest[:2]
        qs, at, fw = rest[2 : 2 + parts], rest[2 + parts : 2 + 2 * parts], rest[2 + 2 * parts :]
        cosine, sine = cos_ref[...], sin_ref[...]

        def joined(column):
            s = slice(column * head_dim, (column + 1) * head_dim)
            total = own_ref[:, s]
            for ref in recv_refs:
                total = total + ref[:, s].astype(F32)
            return total

        def rotate(x):
            return x * cosine + pltpu.roll(x, half, 1) * sine

        contract = (((1,), (1,)), ((), ()))
        column, fresh, new_values = 0, [], []
        for n, (_, first, count) in enumerate(chunk):
            pad = pads[n]
            for h in range(pad):
                value = rotate(joined(column + h)) if h < count else jnp.zeros((tokens, head_dim), F32)
                qs[n][pl.ds(h, tokens, stride=pad), :] = value
            column += count
            if first == 0:
                new_key = rotate(joined(column)).astype(BF16)
                new_value = joined(column + 1).astype(BF16)
                column += 2
            else:
                new_key, new_value = pair_refs[0][...], pair_refs[1][...]
            new_values.append(new_value.astype(F32))
            scores = lax.dot_general(
                qs[n][...].astype(BF16), new_key, contract, preferred_element_type=F32
            )
            row = lax.broadcasted_iota(jnp.int32, scores.shape, 0) // pad
            col = lax.broadcasted_iota(jnp.int32, scores.shape, 1)
            fresh.append(jnp.where((row // 2 == col // 2) & (col <= row), scores * scale, -1e30))
        if keep:
            kept_refs[0][...], kept_refs[1][...] = new_key, new_value

        for r in range(requests):
            q = [qs[n][2 * r * pads[n] : 2 * (r + 1) * pads[n], :].astype(BF16) for n in range(parts)]
            sc[r * rows : (r + 1) * rows, :] = lax.dot_general(
                jnp.concatenate(q, axis=0), k_ref[r], contract, preferred_element_type=F32
            )
        slot = lax.broadcasted_iota(jnp.int32, (1, slots), 1)
        mine = [lax.rem(slot, groups) == g for g, _, _ in chunk]
        for r in range(requests):
            live = slot < len_ref[r] * groups
            for n in range(parts):
                s = slice(r * rows + starts[n], r * rows + starts[n + 1])
                own_rows = slice(2 * r * pads[n], 2 * (r + 1) * pads[n])
                score = jnp.where(live & mine[n], sc[s, :] * scale, -1e30)
                f = fresh[n][own_rows]
                top = jnp.maximum(score.max(axis=1, keepdims=True), f.max(axis=1, keepdims=True))
                e, fe = jnp.exp(score - top), jnp.exp(f - top)
                inverse = 1.0 / (e.sum(axis=1, keepdims=True) + fe.sum(axis=1, keepdims=True))
                wt[s, :] = (e * inverse).astype(BF16)
                fw[n][own_rows, :] = (fe * inverse).astype(BF16).astype(F32)
        for r in range(requests):
            total = dot(wt[r * rows : (r + 1) * rows, :], v_ref[r])
            for n in range(parts):
                own_rows = slice(2 * r * pads[n], 2 * (r + 1) * pads[n])
                value = total[starts[n] : starts[n + 1]]
                for token in (2 * r, 2 * r + 1):
                    value = value + fw[n][own_rows, token : token + 1] * new_values[n][token : token + 1]
                at[n][own_rows, :] = value
        column = 0
        for n, (_, _, count) in enumerate(chunk):
            for h in range(count):
                out_ref[:, column : column + head_dim] = at[n][
                    pl.ds(h, tokens, stride=pads[n]), :
                ].astype(BF16)
                column += head_dim

    heads = sum(count for _, _, count in chunk)
    out_shape = [pltpu.VMEM((tokens, heads * head_dim), BF16)]
    if keep:
        out_shape += [pltpu.VMEM((tokens, head_dim), BF16)] * 2
    per_part = [pltpu.VMEM((tokens * pad, head_dim), F32) for pad in pads]
    return pl.pallas_call(
        kernel,
        out_shape=out_shape,
        in_specs=[IN_VMEM] * (1 + nrecv + npair + 2) + [IN_SMEM] + [IN_VMEM] * 2,
        out_specs=[IN_VMEM] * len(out_shape),
        scratch_shapes=[
            pltpu.VMEM((requests * rows, slots), F32),
            pltpu.VMEM((requests * rows, slots), BF16),
        ]
        + per_part
        + per_part
        + [pltpu.VMEM((tokens * pad, tokens), F32) for pad in pads],
        cost_estimate=cost(1 << 31, 12 << 20),
        compiler_params=pltpu.CompilerParams(vmem_limit_bytes=10 << 20),
        name="attend",
    )(own, *received, *fresh_pairs, keys, values, lengths, cosine, sine)


def project_out(blocks, acc, weight, first, last, ngx, ngy):
    width = weight.shape[1]
    block_rows, depth = blocks[0].shape
    rows = block_rows * ngx
    part = rows // ngy

    def kernel(*refs):
        a_refs, w_ref, rest = refs[:ngx], refs[ngx], refs[ngx + 1 :]
        if acc is not None:
            acc_ref, rest = rest[0], rest[1:]
        outs, rest = (rest[:ngy], rest[ngy:]) if last else (rest[:1], rest[1:])
        xs = rest[0]
        total = rest[1] if last else outs[0]
        me_x, me_y = lax.axis_index("gx"), lax.axis_index("gy")
        for step in range(ngx):
            xs[rows_at(partner(me_x, step, ngx), block_rows), :] = a_refs[step][...]
        for s in column_tiles(width):
            product = dot(xs[...], w_ref[first : first + depth, s])
            total[:, s] = product if acc is None else acc_ref[:, s] + product
        if last:
            outs[0][...] = total[rows_at(me_y, part), :]
            for step in range(1, ngy):
                outs[step][...] = total[rows_at(target(me_y, step, ngy), part), :].astype(BF16)

    if last:
        out_shape = [pltpu.VMEM((part, width), F32)] + [pltpu.VMEM((part, width), BF16)] * (ngy - 1)
    else:
        out_shape = [pltpu.VMEM((rows, width), F32)]
    extra = [] if acc is None else [acc]
    return pl.pallas_call(
        kernel,
        out_shape=out_shape,
        in_specs=[IN_VMEM] * (ngx + 1 + len(extra)),
        out_specs=[IN_VMEM] * len(out_shape),
        scratch_shapes=[pltpu.VMEM((rows, depth), BF16)]
        + ([pltpu.VMEM((rows, width), F32)] if last else []),
        cost_estimate=cost(2 * rows * depth * width, depth * width * 2),
        compiler_params=pltpu.CompilerParams(vmem_limit_bytes=8 << 20),
        name="project_out",
    )(*blocks, weight, *extra)


def finish(own, received):
    rows, width = own.shape

    def kernel(*refs):
        total = refs[0][...]
        for ref in refs[1:-1]:
            total = total + ref[...].astype(F32)
        refs[-1][...] = total.reshape(rows // 2, 2, width).astype(BF16)

    return pl.pallas_call(
        kernel,
        out_shape=jax.ShapeDtypeStruct((rows // 2, 2, width), BF16),
        in_specs=[IN_VMEM] * (1 + len(received)),
        out_specs=IN_VMEM,
        compiler_params=pltpu.CompilerParams(vmem_limit_bytes=8 << 20),
        name="finish",
    )(own, *received)


def frequencies_of(head_dim):
    half = np.exp(
        np.arange(head_dim // 2, dtype=np.float32)
        * np.float32(-2.0 * math.log(500000.0) / head_dim)
    ).astype(np.float32)
    return jnp.asarray(np.concatenate([half, half])[None])


def on_device(
    ngx, ngy, hidden_in, joined_projection_weight, w_out, key_cache, cached_value_rows, lengths, positions
):
    requests, cache_len, groups, head_dim = key_cache.shape
    keys = key_cache.reshape(requests, cache_len * groups, head_dim)
    values = cached_value_rows.reshape(requests, cache_len * groups, head_dim)
    per_group = joined_projection_weight.shape[1] // (groups * head_dim) - 2
    chunks = chunks_of(groups, per_group)
    ranges = [ranges_of(chunk, per_group, head_dim) for chunk in chunks]
    widths = [sum(width for _, width in r) for r in ranges]

    rows = [hidden_in] + [swap(hidden_in, "gy", s, ngy) for s in range(1, ngy)]
    near, cosine, sine = fetch(
        joined_projection_weight,
        cut(ranges[0], 0, max(head_dim, widths[0] * 9 // 10 // 256 * 256)),
        positions,
        frequencies_of(head_dim),
    )
    joined = []
    for n in range(len(chunks)):
        last = n == len(chunks) - 1
        coming = [] if last else cut(ranges[n + 1], 0, max(head_dim, widths[n + 1] // 256 * 256))
        made = project(rows, near, joined_projection_weight, ranges[n], coming, ngx, ngy)
        joined.append((made[0], [swap(made[s], "gx", s, ngx) for s in range(1, ngx)]))
        if not last:
            near = made[ngx]
        if len(rows) > 1:
            rows = [made[-1]]

    attended, pair = [], []
    for n, chunk in enumerate(chunks):
        own, received = joined[n]
        keep = n + 1 < len(chunks) and chunks[n + 1][0][1] > 0
        mine, *pair = attend(
            own, received, pair, keys, values, lengths, cosine, sine, chunk, keep, groups
        )
        attended.append([mine] + [swap(mine, "gx", s, ngx) for s in range(1, ngx)])
    total, first = None, 0
    for n in range(len(chunks)):
        made = project_out(attended[n], total, w_out, first, n == len(chunks) - 1, ngx, ngy)
        first += attended[n][0].shape[1]
        total = made[0]
    return finish(made[0], [swap(made[s], "gy", s, ngy) for s in range(1, ngy)])


def solution(mesh):
    in_specs = (
        P(("groups", "gy"), None, "gx"),
        P("gx", "gy"),
        P("gy", "gx"),
        P(("groups", "gx"), None, "gy", None),
        P(("groups", "gx"), None, "gy", None),
        P(("groups", "gx")),
        P(("groups", "gx")),
    )
    out_specs = P(("groups", "gy"), None, "gx")
    return jax.shard_map(
        functools.partial(on_device, mesh.shape["gx"], mesh.shape["gy"]),
        mesh=mesh,
        in_specs=in_specs,
        out_specs=out_specs,
        check_vma=False,
    )
```

```python
import functools
import math

import jax
import jax.numpy as jnp
import numpy as np
from jax import lax
from jax.experimental import pallas as pl
from jax.experimental.pallas import tpu as pltpu
from jax.sharding import PartitionSpec as P

BF16 = jnp.bfloat16
F32 = jnp.float32
IN_VMEM = pl.BlockSpec(memory_space=pltpu.VMEM)
IN_SMEM = pl.BlockSpec(memory_space=pltpu.SMEM)
ANYWHERE = pl.BlockSpec(memory_space=pl.ANY)
PIECES = 4


def partner(index, step, count):
    if count & (count - 1) == 0:
        return index ^ step
    return lax.rem(index + count - step, count) if not isinstance(index, int) else (index - step) % count


def target(index, step, count):
    if count & (count - 1) == 0:
        return index ^ step
    return lax.rem(index + step, count) if not isinstance(index, int) else (index + step) % count


def swap(block, axis, step, count):
    return lax.ppermute(block, axis, [(i, target(i, step, count)) for i in range(count)])


def order_of(count):
    return [*range(count // 2, count), *range(1, count // 2)] if count > 2 else [*range(1, count)]


def hbm(array):
    return pltpu.with_memory_space_constraint(array, pltpu.HBM)


def vmem(array):
    return pltpu.with_memory_space_constraint(array, pltpu.VMEM)


def rows_at(index, count):
    return pl.ds(pl.multiple_of(index * count, count), count)


def dot(x, w):
    return jnp.dot(x, w, preferred_element_type=F32)


def column_tiles(width, tile=512):
    return [slice(c, min(c + tile, width)) for c in range(0, width, tile)]


def columns_in_two_steps(width, body):
    half = width // 2

    if width % 256:
        for s in column_tiles(width):
            body(pl.ds(s.start, s.stop - s.start))
        return

    @pl.loop(0, 2)
    def _(step):
        for s in column_tiles(half):
            body(pl.ds(pl.multiple_of(step * half + s.start, 128), s.stop - s.start))


def cost(flops, read):
    return pl.CostEstimate(flops=flops, bytes_accessed=read, transcendentals=0)


def chunks_of(groups, per_group, small=8):
    if per_group <= small:
        return [[(g, 0, per_group)] for g in range(groups)]
    first = [(g, 0, per_group) for g in range(groups - 1)] + [(groups - 1, 0, per_group - small)]
    return [first, [(groups - 1, per_group - small, small)]]


def ranges_of(chunk, per_group, unit):
    made = []
    for g, first, count in chunk:
        base = g * (per_group + 2)
        made.append([base + first, count])
        if first == 0:
            made.append([base + per_group, 2])
    merged = []
    for first, count in made:
        if merged and merged[-1][0] + merged[-1][1] == first:
            merged[-1][1] += count
        else:
            merged.append([first, count])
    return [(first * unit, count * unit) for first, count in merged]


def cut(ranges, begin, end):
    made, at = [], 0
    for first, width in ranges:
        low, high = max(begin, at), min(end, at + width)
        if low < high:
            made.append((first + low - at, low - begin, high - low))
        at += width
    return made


def copy_columns(w_ref, to, parts, sems):
    piece = w_ref.shape[0] // PIECES
    made = []
    for n, (source, place, width) in enumerate(parts):
        for i in range(PIECES):
            rows = pl.ds(i * piece, piece)
            copy = pltpu.make_async_copy(
                w_ref.at[rows, pl.ds(source, width)], to.at[rows, pl.ds(place, width)], sems.at[n, i]
            )
            copy.start()
            made.append(copy)
    return made


def fetch(weight, parts, positions, frequencies):
    depth = weight.shape[0]
    width = sum(part[2] for part in parts)
    requests, head_dim = positions.shape[0], frequencies.shape[1]

    def kernel(w_ref, pos_any, freq_any, near_ref, cos_ref, sin_ref, pos_ref, freq_ref, w_sems, s_sems):
        small = [
            pltpu.make_async_copy(pos_any, pos_ref, s_sems.at[0]),
            pltpu.make_async_copy(freq_any, freq_ref, s_sems.at[1]),
        ]
        for copy in small:
            copy.start()
        copies = copy_columns(w_ref, near_ref, parts, w_sems)
        for copy in small:
            copy.wait()
        row = lax.broadcasted_iota(jnp.int32, (2 * requests, head_dim), 0)
        place = row % 2
        for r in range(requests):
            place = place + jnp.where(row // 2 == r, pos_ref[r], 0)
        turned = place.astype(F32) * freq_ref[...]
        lane = lax.broadcasted_iota(jnp.int32, (2 * requests, head_dim), 1)
        cos_ref[...] = jnp.cos(turned)
        sine = jnp.sin(turned)
        sin_ref[...] = jnp.where(lane < head_dim // 2, -sine, sine)
        for copy in copies:
            copy.wait()

    angle = pltpu.VMEM((2 * requests, head_dim), F32)
    return pl.pallas_call(
        kernel,
        out_shape=[pltpu.VMEM((depth, width), weight.dtype), angle, angle],
        in_specs=[ANYWHERE] * 3,
        out_specs=[IN_VMEM] * 3,
        scratch_shapes=[
            pltpu.SMEM((requests,), jnp.int32),
            pltpu.VMEM((1, head_dim), F32),
            pltpu.SemaphoreType.DMA((len(parts), PIECES)),
            pltpu.SemaphoreType.DMA((2,)),
        ],
        cost_estimate=cost(0, 4 * depth * width),
        compiler_params=pltpu.CompilerParams(vmem_limit_bytes=4 << 20),
        name="fetch",
    )(hbm(weight), hbm(positions), hbm(frequencies))


def project(blocks, near, weight, ranges, coming, ngx, ngy):
    depth, ready = near.shape
    width = sum(count for _, count in ranges)
    late_tiles = column_tiles(width - ready, 256)
    late_parts = [cut(ranges, ready + t.start, ready + t.stop) for t in late_tiles]
    ahead = sum(part[2] for part in coming)
    count = len(blocks)
    rows = 2 * blocks[0].shape[0] * ngy if count > 1 else blocks[0].shape[0]
    part = rows // ngx

    def kernel(*refs):
        x_refs, (near_ref, w_ref, own_ref), rest = refs[:count], refs[count : count + 3], refs[count + 3 :]
        send_refs, rest = rest[: ngx - 1], rest[ngx - 1 :]
        if ahead:
            next_ref, rest = rest[0], rest[1:]
        if count > 1:
            xs, rest = rest[0], rest[1:]
        else:
            xs = x_refs[0]
        total, rest = rest[0], rest[1:]
        late_copies = []
        if late_tiles:
            late, late_sems, rest = rest[0], rest[1], rest[2:]
            late_copies = [
                copy_columns(w_ref, late.at[:, pl.ds(t.start, t.stop - t.start)], parts, late_sems.at[i])
                for i, (t, parts) in enumerate(zip(late_tiles, late_parts))
            ]
        next_copies = copy_columns(w_ref, next_ref, coming, rest[0]) if ahead else []
        me_x, me_y = lax.axis_index("gx"), lax.axis_index("gy")
        if count > 1:
            for step in range(ngy):
                xs[rows_at(partner(me_y, step, ngy), rows // ngy), :] = x_refs[step][...].reshape(
                    rows // ngy, depth
                )

        def product(s):
            total[:, s] = dot(xs[...], near_ref[:, s])

        columns_in_two_steps(ready, product)
        for s, arriving in zip(late_tiles, late_copies):
            for copy in arriving:
                copy.wait()
            total[:, ready + s.start : ready + s.stop] = dot(xs[...], late[:, s])
        own_ref[...] = total[rows_at(me_x, part), :]
        for step in range(1, ngx):
            send_refs[step - 1][...] = total[rows_at(target(me_x, step, ngx), part), :].astype(BF16)
        for copy in next_copies:
            copy.wait()

    out_shape = [pltpu.VMEM((part, width), F32)] + [pltpu.VMEM((part, width), BF16)] * (ngx - 1)
    if ahead:
        out_shape.append(pltpu.VMEM((depth, ahead), weight.dtype))
    if count > 1:
        out_shape.append(pltpu.VMEM((rows, depth), BF16))
    scratch = [pltpu.VMEM((rows, width), F32)]
    if late_tiles:
        scratch.append(pltpu.VMEM((depth, width - ready), weight.dtype))
        most = max(len(parts) for parts in late_parts)
        scratch.append(pltpu.SemaphoreType.DMA((len(late_tiles), most, PIECES)))
    if ahead:
        scratch.append(pltpu.SemaphoreType.DMA((len(coming), PIECES)))
    return pl.pallas_call(
        kernel,
        out_shape=out_shape,
        in_specs=[IN_VMEM] * (count + 1) + [ANYWHERE],
        out_specs=[IN_VMEM] * len(out_shape),
        scratch_shapes=scratch,
        cost_estimate=cost(2 * rows * depth * width, 2 * depth * width),
        compiler_params=pltpu.CompilerParams(vmem_limit_bytes=14 << 20),
        name="project",
    )(*blocks, vmem(near), hbm(weight))


def attend(own, received, fresh_pairs, keys, values, lengths, cosine, sine, chunk, keep, groups):
    tokens = own.shape[0]
    requests, slots, head_dim = keys.shape
    half = head_dim // 2
    scale = 1.0 / math.sqrt(head_dim)
    nrecv, npair = len(received), len(fresh_pairs)
    pads = [-(-count // 8) * 8 for _, _, count in chunk]
    starts = [2 * sum(pads[:i]) for i in range(len(pads) + 1)]
    rows, parts = starts[-1], len(chunk)

    def kernel(*refs):
        own_ref, recv_refs, rest = refs[0], refs[1 : 1 + nrecv], refs[1 + nrecv :]
        pair_refs, rest = rest[:npair], rest[npair:]
        k_ref, v_ref, len_ref, cos_ref, sin_ref, out_ref = rest[:6]
        kept_refs, rest = (rest[6:8], rest[8:]) if keep else ((), rest[6:])
        sc, wt = rest[:2]
        qs, at, fw = rest[2 : 2 + parts], rest[2 + parts : 2 + 2 * parts], rest[2 + 2 * parts :]
        cosine, sine = cos_ref[...], sin_ref[...]

        def joined(column):
            s = slice(column * head_dim, (column + 1) * head_dim)
            total = own_ref[:, s]
            for ref in recv_refs:
                total = total + ref[:, s].astype(F32)
            return total

        def rotate(x):
            return x * cosine + pltpu.roll(x, half, 1) * sine

        contract = (((1,), (1,)), ((), ()))
        column, fresh, new_values = 0, [], []
        for n, (_, first, count) in enumerate(chunk):
            pad = pads[n]
            for h in range(pad):
                value = rotate(joined(column + h)) if h < count else jnp.zeros((tokens, head_dim), F32)
                qs[n][pl.ds(h, tokens, stride=pad), :] = value
            column += count
            if first == 0:
                new_key = rotate(joined(column)).astype(BF16)
                new_value = joined(column + 1).astype(BF16)
                column += 2
            else:
                new_key, new_value = pair_refs[0][...], pair_refs[1][...]
            new_values.append(new_value.astype(F32))
            scores = lax.dot_general(
                qs[n][...].astype(BF16), new_key, contract, preferred_element_type=F32
            )
            row = lax.broadcasted_iota(jnp.int32, scores.shape, 0) // pad
            col = lax.broadcasted_iota(jnp.int32, scores.shape, 1)
            fresh.append(jnp.where((row // 2 == col // 2) & (col <= row), scores * scale, -1e30))
        if keep:
            kept_refs[0][...], kept_refs[1][...] = new_key, new_value

        for r in range(requests):
            q = [qs[n][2 * r * pads[n] : 2 * (r + 1) * pads[n], :].astype(BF16) for n in range(parts)]
            sc[r * rows : (r + 1) * rows, :] = lax.dot_general(
                jnp.concatenate(q, axis=0), k_ref[r], contract, preferred_element_type=F32
            )
        slot = lax.broadcasted_iota(jnp.int32, (1, slots), 1)
        mine = [lax.rem(slot, groups) == g for g, _, _ in chunk]
        for r in range(requests):
            live = slot < len_ref[r] * groups
            for n in range(parts):
                s = slice(r * rows + starts[n], r * rows + starts[n + 1])
                own_rows = slice(2 * r * pads[n], 2 * (r + 1) * pads[n])
                score = jnp.where(live & mine[n], sc[s, :] * scale, -1e30)
                f = fresh[n][own_rows]
                top = jnp.maximum(score.max(axis=1, keepdims=True), f.max(axis=1, keepdims=True))
                e, fe = jnp.exp(score - top), jnp.exp(f - top)
                inverse = 1.0 / (e.sum(axis=1, keepdims=True) + fe.sum(axis=1, keepdims=True))
                wt[s, :] = (e * inverse).astype(BF16)
                fw[n][own_rows, :] = (fe * inverse).astype(BF16).astype(F32)
        for r in range(requests):
            total = dot(wt[r * rows : (r + 1) * rows, :], v_ref[r])
            for n in range(parts):
                own_rows = slice(2 * r * pads[n], 2 * (r + 1) * pads[n])
                value = total[starts[n] : starts[n + 1]]
                for token in (2 * r, 2 * r + 1):
                    value = value + fw[n][own_rows, token : token + 1] * new_values[n][token : token + 1]
                at[n][own_rows, :] = value
        column = 0
        for n, (_, _, count) in enumerate(chunk):
            for h in range(count):
                out_ref[:, column : column + head_dim] = at[n][
                    pl.ds(h, tokens, stride=pads[n]), :
                ].astype(BF16)
                column += head_dim

    heads = sum(count for _, _, count in chunk)
    out_shape = [pltpu.VMEM((tokens, heads * head_dim), BF16)]
    if keep:
        out_shape += [pltpu.VMEM((tokens, head_dim), BF16)] * 2
    per_part = [pltpu.VMEM((tokens * pad, head_dim), F32) for pad in pads]
    return pl.pallas_call(
        kernel,
        out_shape=out_shape,
        in_specs=[IN_VMEM] * (1 + nrecv + npair + 2) + [IN_SMEM] + [IN_VMEM] * 2,
        out_specs=[IN_VMEM] * len(out_shape),
        scratch_shapes=[
            pltpu.VMEM((requests * rows, slots), F32),
            pltpu.VMEM((requests * rows, slots), BF16),
        ]
        + per_part
        + per_part
        + [pltpu.VMEM((tokens * pad, tokens), F32) for pad in pads],
        cost_estimate=cost(1 << 31, 12 << 20),
        compiler_params=pltpu.CompilerParams(vmem_limit_bytes=10 << 20),
        name="attend",
    )(own, *received, *fresh_pairs, keys, values, lengths, cosine, sine)


def project_out(blocks, acc, weight, first, last, ngx, ngy):
    width = weight.shape[1]
    block_rows, depth = blocks[0].shape
    rows = block_rows * ngx
    part = rows // ngy

    def kernel(*refs):
        a_refs, w_ref, rest = refs[:ngx], refs[ngx], refs[ngx + 1 :]
        if acc is not None:
            acc_ref, rest = rest[0], rest[1:]
        outs, rest = (rest[:ngy], rest[ngy:]) if last else (rest[:1], rest[1:])
        xs = rest[0]
        total = rest[1] if last else outs[0]
        me_x, me_y = lax.axis_index("gx"), lax.axis_index("gy")
        for step in range(ngx):
            xs[rows_at(partner(me_x, step, ngx), block_rows), :] = a_refs[step][...]
        for s in column_tiles(width):
            product = dot(xs[...], w_ref[first : first + depth, s])
            total[:, s] = product if acc is None else acc_ref[:, s] + product
        if last:
            outs[0][...] = total[rows_at(me_y, part), :]
            for step in range(1, ngy):
                outs[step][...] = total[rows_at(target(me_y, step, ngy), part), :].astype(BF16)

    if last:
        out_shape = [pltpu.VMEM((part, width), F32)] + [pltpu.VMEM((part, width), BF16)] * (ngy - 1)
    else:
        out_shape = [pltpu.VMEM((rows, width), F32)]
    extra = [] if acc is None else [acc]
    return pl.pallas_call(
        kernel,
        out_shape=out_shape,
        in_specs=[IN_VMEM] * (ngx + 1 + len(extra)),
        out_specs=[IN_VMEM] * len(out_shape),
        scratch_shapes=[pltpu.VMEM((rows, depth), BF16)]
        + ([pltpu.VMEM((rows, width), F32)] if last else []),
        cost_estimate=cost(2 * rows * depth * width, depth * width * 2),
        compiler_params=pltpu.CompilerParams(vmem_limit_bytes=8 << 20),
        name="project_out",
    )(*blocks, weight, *extra)


def finish(own, received):
    rows, width = own.shape

    def kernel(*refs):
        total = refs[0][...]
        for ref in refs[1:-1]:
            total = total + ref[...].astype(F32)
        refs[-1][...] = total.reshape(rows // 2, 2, width).astype(BF16)

    return pl.pallas_call(
        kernel,
        out_shape=jax.ShapeDtypeStruct((rows // 2, 2, width), BF16),
        in_specs=[IN_VMEM] * (1 + len(received)),
        out_specs=IN_VMEM,
        compiler_params=pltpu.CompilerParams(vmem_limit_bytes=8 << 20),
        name="finish",
    )(own, *received)


def frequencies_of(head_dim):
    half = np.exp(
        np.arange(head_dim // 2, dtype=np.float32)
        * np.float32(-2.0 * math.log(500000.0) / head_dim)
    ).astype(np.float32)
    return jnp.asarray(np.concatenate([half, half])[None])


def on_device(
    ngx, ngy, hidden_in, joined_projection_weight, w_out, key_cache, cached_value_rows, lengths, positions
):
    requests, cache_len, groups, head_dim = key_cache.shape
    keys = key_cache.reshape(requests, cache_len * groups, head_dim)
    values = cached_value_rows.reshape(requests, cache_len * groups, head_dim)
    per_group = joined_projection_weight.shape[1] // (groups * head_dim) - 2
    chunks = chunks_of(groups, per_group)
    ranges = [ranges_of(chunk, per_group, head_dim) for chunk in chunks]
    widths = [sum(width for _, width in r) for r in ranges]

    rows = [hidden_in] + [swap(hidden_in, "gy", s, ngy) for s in range(1, ngy)]
    near, cosine, sine = fetch(
        joined_projection_weight,
        cut(ranges[0], 0, max(head_dim, widths[0] * 9 // 10 // 256 * 256)),
        positions,
        frequencies_of(head_dim),
    )
    joined = []
    for n in range(len(chunks)):
        last = n == len(chunks) - 1
        coming = [] if last else cut(ranges[n + 1], 0, max(head_dim, widths[n + 1] // 256 * 256))
        made = project(rows, near, joined_projection_weight, ranges[n], coming, ngx, ngy)
        joined.append((made[0], [swap(made[s], "gx", s, ngx) for s in order_of(ngx)]))
        if not last:
            near = made[ngx]
        if len(rows) > 1:
            rows = [made[-1]]

    attended, pair = [], []
    for n, chunk in enumerate(chunks):
        own, received = joined[n]
        keep = n + 1 < len(chunks) and chunks[n + 1][0][1] > 0
        mine, *pair = attend(
            own, received, pair, keys, values, lengths, cosine, sine, chunk, keep, groups
        )
        attended.append([mine] + [swap(mine, "gx", s, ngx) for s in range(1, ngx)])
    total, first = None, 0
    for n in range(len(chunks)):
        made = project_out(attended[n], total, w_out, first, n == len(chunks) - 1, ngx, ngy)
        first += attended[n][0].shape[1]
        total = made[0]
    return finish(made[0], [swap(made[s], "gy", s, ngy) for s in order_of(ngy)])


def solution(mesh):
    in_specs = (
        P(("groups", "gy"), None, "gx"),
        P("gx", "gy"),
        P("gy", "gx"),
        P(("groups", "gx"), None, "gy", None),
        P(("groups", "gx"), None, "gy", None),
        P(("groups", "gx")),
        P(("groups", "gx")),
    )
    out_specs = P(("groups", "gy"), None, "gx")
    return jax.shard_map(
        functools.partial(on_device, mesh.shape["gx"], mesh.shape["gy"]),
        mesh=mesh,
        in_specs=in_specs,
        out_specs=out_specs,
        check_vma=False,
    )
```

```python
import functools
import math

import jax
import jax.numpy as jnp
import numpy as np
from jax import lax
from jax.experimental import pallas as pl
from jax.experimental.pallas import tpu as pltpu
from jax.sharding import PartitionSpec as P

BF16 = jnp.bfloat16
F32 = jnp.float32
IN_VMEM = pl.BlockSpec(memory_space=pltpu.VMEM)
IN_SMEM = pl.BlockSpec(memory_space=pltpu.SMEM)
ANYWHERE = pl.BlockSpec(memory_space=pl.ANY)
PIECES = 4


def partner(index, step, count):
    if count & (count - 1) == 0:
        return index ^ step
    return lax.rem(index + count - step, count) if not isinstance(index, int) else (index - step) % count


def target(index, step, count):
    if count & (count - 1) == 0:
        return index ^ step
    return lax.rem(index + step, count) if not isinstance(index, int) else (index + step) % count


def swap(block, axis, step, count):
    return lax.ppermute(block, axis, [(i, target(i, step, count)) for i in range(count)])


def order_of(count):
    return [*range(count // 2, count), *range(1, count // 2)] if count > 2 else [*range(1, count)]


def hbm(array):
    return pltpu.with_memory_space_constraint(array, pltpu.HBM)


def vmem(array):
    return pltpu.with_memory_space_constraint(array, pltpu.VMEM)


def rows_at(index, count):
    return pl.ds(pl.multiple_of(index * count, count), count)


def dot(x, w):
    return jnp.dot(x, w, preferred_element_type=F32)


def column_tiles(width, tile=512):
    return [slice(c, min(c + tile, width)) for c in range(0, width, tile)]


def columns_in_two_steps(width, body):
    half = width // 2

    if width % 256:
        for s in column_tiles(width):
            body(pl.ds(s.start, s.stop - s.start))
        return

    @pl.loop(0, 2)
    def _(step):
        for s in column_tiles(half):
            body(pl.ds(pl.multiple_of(step * half + s.start, 128), s.stop - s.start))


def cost(flops, read):
    return pl.CostEstimate(flops=flops, bytes_accessed=read, transcendentals=0)


def chunks_of(groups, per_group, small=8):
    if per_group <= small:
        return [[(g, 0, per_group)] for g in range(groups)]
    first = [(g, 0, per_group) for g in range(groups - 1)] + [(groups - 1, 0, per_group - small)]
    return [first, [(groups - 1, per_group - small, small)]]


def ranges_of(chunk, per_group, unit):
    made = []
    for g, first, count in chunk:
        base = g * (per_group + 2)
        made.append([base + first, count])
        if first == 0:
            made.append([base + per_group, 2])
    merged = []
    for first, count in made:
        if merged and merged[-1][0] + merged[-1][1] == first:
            merged[-1][1] += count
        else:
            merged.append([first, count])
    return [(first * unit, count * unit) for first, count in merged]


def cut(ranges, begin, end):
    made, at = [], 0
    for first, width in ranges:
        low, high = max(begin, at), min(end, at + width)
        if low < high:
            made.append((first + low - at, low - begin, high - low))
        at += width
    return made


def copy_columns(w_ref, to, parts, sems):
    piece = w_ref.shape[0] // PIECES
    made = []
    for n, (source, place, width) in enumerate(parts):
        for i in range(PIECES):
            rows = pl.ds(i * piece, piece)
            copy = pltpu.make_async_copy(
                w_ref.at[rows, pl.ds(source, width)], to.at[rows, pl.ds(place, width)], sems.at[n, i]
            )
            copy.start()
            made.append(copy)
    return made


def fetch(weight, parts, positions, frequencies):
    depth = weight.shape[0]
    width = sum(part[2] for part in parts)
    requests, head_dim = positions.shape[0], frequencies.shape[1]

    def kernel(w_ref, pos_any, freq_any, near_ref, cos_ref, sin_ref, pos_ref, freq_ref, w_sems, s_sems):
        small = [
            pltpu.make_async_copy(pos_any, pos_ref, s_sems.at[0]),
            pltpu.make_async_copy(freq_any, freq_ref, s_sems.at[1]),
        ]
        for copy in small:
            copy.start()
        copies = copy_columns(w_ref, near_ref, parts, w_sems)
        for copy in small:
            copy.wait()
        row = lax.broadcasted_iota(jnp.int32, (2 * requests, head_dim), 0)
        place = row % 2
        for r in range(requests):
            place = place + jnp.where(row // 2 == r, pos_ref[r], 0)
        turned = place.astype(F32) * freq_ref[...]
        lane = lax.broadcasted_iota(jnp.int32, (2 * requests, head_dim), 1)
        cos_ref[...] = jnp.cos(turned)
        sine = jnp.sin(turned)
        sin_ref[...] = jnp.where(lane < head_dim // 2, -sine, sine)
        for copy in copies:
            copy.wait()

    angle = pltpu.VMEM((2 * requests, head_dim), F32)
    return pl.pallas_call(
        kernel,
        out_shape=[pltpu.VMEM((depth, width), weight.dtype), angle, angle],
        in_specs=[ANYWHERE] * 3,
        out_specs=[IN_VMEM] * 3,
        scratch_shapes=[
            pltpu.SMEM((requests,), jnp.int32),
            pltpu.VMEM((1, head_dim), F32),
            pltpu.SemaphoreType.DMA((len(parts), PIECES)),
            pltpu.SemaphoreType.DMA((2,)),
        ],
        cost_estimate=cost(0, 4 * depth * width),
        compiler_params=pltpu.CompilerParams(vmem_limit_bytes=4 << 20),
        name="fetch",
    )(hbm(weight), hbm(positions), hbm(frequencies))


def project(blocks, near, weight, ranges, coming, ngx, ngy):
    depth, ready = near.shape
    width = sum(count for _, count in ranges)
    late_tiles = column_tiles(width - ready)
    late_parts = [cut(ranges, ready + t.start, ready + t.stop) for t in late_tiles]
    ahead = sum(part[2] for part in coming)
    count = len(blocks)
    rows = 2 * blocks[0].shape[0] * ngy if count > 1 else blocks[0].shape[0]
    part = rows // ngx

    def kernel(*refs):
        x_refs, (near_ref, w_ref, own_ref), rest = refs[:count], refs[count : count + 3], refs[count + 3 :]
        send_refs, rest = rest[: ngx - 1], rest[ngx - 1 :]
        if ahead:
            next_ref, rest = rest[0], rest[1:]
        if count > 1:
            xs, rest = rest[0], rest[1:]
        else:
            xs = x_refs[0]
        total, rest = rest[0], rest[1:]
        late_copies = []
        if late_tiles:
            late, late_sems, rest = rest[0], rest[1], rest[2:]
            late_copies = [
                copy_columns(w_ref, late.at[:, pl.ds(t.start, t.stop - t.start)], parts, late_sems.at[i])
                for i, (t, parts) in enumerate(zip(late_tiles, late_parts))
            ]
        next_copies = copy_columns(w_ref, next_ref, coming, rest[0]) if ahead else []
        me_x, me_y = lax.axis_index("gx"), lax.axis_index("gy")
        if count > 1:
            for step in range(ngy):
                xs[rows_at(partner(me_y, step, ngy), rows // ngy), :] = x_refs[step][...].reshape(
                    rows // ngy, depth
                )

        def product(s):
            total[:, s] = dot(xs[...], near_ref[:, s])

        columns_in_two_steps(ready, product)
        for s, arriving in zip(late_tiles, late_copies):
            for copy in arriving:
                copy.wait()
            total[:, ready + s.start : ready + s.stop] = dot(xs[...], late[:, s])
        own_ref[...] = total[rows_at(me_x, part), :]
        for step in range(1, ngx):
            send_refs[step - 1][...] = total[rows_at(target(me_x, step, ngx), part), :].astype(BF16)
        for copy in next_copies:
            copy.wait()

    out_shape = [pltpu.VMEM((part, width), F32)] + [pltpu.VMEM((part, width), BF16)] * (ngx - 1)
    if ahead:
        out_shape.append(pltpu.VMEM((depth, ahead), weight.dtype))
    if count > 1:
        out_shape.append(pltpu.VMEM((rows, depth), BF16))
    scratch = [pltpu.VMEM((rows, width), F32)]
    if late_tiles:
        scratch.append(pltpu.VMEM((depth, width - ready), weight.dtype))
        most = max(len(parts) for parts in late_parts)
        scratch.append(pltpu.SemaphoreType.DMA((len(late_tiles), most, PIECES)))
    if ahead:
        scratch.append(pltpu.SemaphoreType.DMA((len(coming), PIECES)))
    return pl.pallas_call(
        kernel,
        out_shape=out_shape,
        in_specs=[IN_VMEM] * (count + 1) + [ANYWHERE],
        out_specs=[IN_VMEM] * len(out_shape),
        scratch_shapes=scratch,
        cost_estimate=cost(2 * rows * depth * width, 2 * depth * width),
        compiler_params=pltpu.CompilerParams(vmem_limit_bytes=14 << 20),
        name="project",
    )(*blocks, vmem(near), hbm(weight))


def attend(own, received, fresh_pairs, keys, values, lengths, cosine, sine, chunk, keep, groups):
    tokens = own.shape[0]
    requests, slots, head_dim = keys.shape
    half = head_dim // 2
    scale = 1.0 / math.sqrt(head_dim)
    nrecv, npair = len(received), len(fresh_pairs)
    pads = [-(-count // 8) * 8 for _, _, count in chunk]
    starts = [2 * sum(pads[:i]) for i in range(len(pads) + 1)]
    rows, parts = starts[-1], len(chunk)

    def kernel(*refs):
        own_ref, recv_refs, rest = refs[0], refs[1 : 1 + nrecv], refs[1 + nrecv :]
        pair_refs, rest = rest[:npair], rest[npair:]
        k_ref, v_ref, len_ref, cos_ref, sin_ref, out_ref = rest[:6]
        kept_refs, rest = (rest[6:8], rest[8:]) if keep else ((), rest[6:])
        sc, wt = rest[:2]
        qs, at, fw = rest[2 : 2 + parts], rest[2 + parts : 2 + 2 * parts], rest[2 + 2 * parts :]
        cosine, sine = cos_ref[...], sin_ref[...]

        def joined(column):
            s = slice(column * head_dim, (column + 1) * head_dim)
            total = own_ref[:, s]
            for ref in recv_refs:
                total = total + ref[:, s].astype(F32)
            return total

        def rotate(x):
            return x * cosine + pltpu.roll(x, half, 1) * sine

        contract = (((1,), (1,)), ((), ()))
        column, new_keys, new_values = 0, [], []
        for n, (_, first, count) in enumerate(chunk):
            pad = pads[n]
            for h in range(pad):
                value = rotate(joined(column + h)) if h < count else jnp.zeros((tokens, head_dim), F32)
                qs[n][pl.ds(h, tokens, stride=pad), :] = value
            column += count
            if first == 0:
                new_key = rotate(joined(column)).astype(BF16)
                new_value = joined(column + 1).astype(BF16)
                column += 2
            else:
                new_key, new_value = pair_refs[0][...], pair_refs[1][...]
            new_values.append(new_value.astype(F32))
            new_keys.append(new_key.astype(F32))
        if keep:
            kept_refs[0][...], kept_refs[1][...] = new_key, new_value

        for r in range(requests):
            q = [qs[n][2 * r * pads[n] : 2 * (r + 1) * pads[n], :].astype(BF16) for n in range(parts)]
            sc[r * rows : (r + 1) * rows, :] = lax.dot_general(
                jnp.concatenate(q, axis=0), k_ref[r], contract, preferred_element_type=F32
            )
        slot = lax.broadcasted_iota(jnp.int32, (1, slots), 1)
        mine = [lax.rem(slot, groups) == g for g, _, _ in chunk]
        for r in range(requests):
            live = slot < len_ref[r] * groups
            for n in range(parts):
                s = slice(r * rows + starts[n], r * rows + starts[n + 1])
                own_rows = slice(2 * r * pads[n], 2 * (r + 1) * pads[n])
                score = jnp.where(live & mine[n], sc[s, :] * scale, -1e30)
                q = qs[n][own_rows, :].astype(BF16).astype(F32)
                second = lax.broadcasted_iota(jnp.int32, (2 * pads[n], 1), 0) >= pads[n]
                f = [
                    (q * new_keys[n][token : token + 1]).sum(axis=1, keepdims=True) * scale
                    for token in (2 * r, 2 * r + 1)
                ]
                f[1] = jnp.where(second, f[1], -1e30)
                top = jnp.maximum(score.max(axis=1, keepdims=True), jnp.maximum(f[0], f[1]))
                e, fe = jnp.exp(score - top), [jnp.exp(x - top) for x in f]
                inverse = 1.0 / (e.sum(axis=1, keepdims=True) + (fe[0] + fe[1]))
                wt[s, :] = (e * inverse).astype(BF16)
                fw[n][own_rows, :] = sum(
                    (x * inverse).astype(BF16).astype(F32) * new_values[n][token : token + 1]
                    for x, token in zip(fe, (2 * r, 2 * r + 1))
                )
        for r in range(requests):
            total = dot(wt[r * rows : (r + 1) * rows, :], v_ref[r])
            for n in range(parts):
                own_rows = slice(2 * r * pads[n], 2 * (r + 1) * pads[n])
                at[n][own_rows, :] = total[starts[n] : starts[n + 1]] + fw[n][own_rows, :]
        column = 0
        for n, (_, _, count) in enumerate(chunk):
            for h in range(count):
                out_ref[:, column : column + head_dim] = at[n][
                    pl.ds(h, tokens, stride=pads[n]), :
                ].astype(BF16)
                column += head_dim

    heads = sum(count for _, _, count in chunk)
    out_shape = [pltpu.VMEM((tokens, heads * head_dim), BF16)]
    if keep:
        out_shape += [pltpu.VMEM((tokens, head_dim), BF16)] * 2
    per_part = [pltpu.VMEM((tokens * pad, head_dim), F32) for pad in pads]
    return pl.pallas_call(
        kernel,
        out_shape=out_shape,
        in_specs=[IN_VMEM] * (1 + nrecv + npair + 2) + [IN_SMEM] + [IN_VMEM] * 2,
        out_specs=[IN_VMEM] * len(out_shape),
        scratch_shapes=[
            pltpu.VMEM((requests * rows, slots), F32),
            pltpu.VMEM((requests * rows, slots), BF16),
        ]
        + per_part
        + per_part
        + per_part,
        cost_estimate=cost(1 << 31, 12 << 20),
        compiler_params=pltpu.CompilerParams(vmem_limit_bytes=10 << 20),
        name="attend",
    )(own, *received, *fresh_pairs, keys, values, lengths, cosine, sine)


def project_out(blocks, acc, weight, first, last, ngx, ngy):
    width = weight.shape[1]
    block_rows, depth = blocks[0].shape
    rows = block_rows * ngx
    part = rows // ngy

    def kernel(*refs):
        a_refs, w_ref, rest = refs[:ngx], refs[ngx], refs[ngx + 1 :]
        if acc is not None:
            acc_ref, rest = rest[0], rest[1:]
        outs, rest = (rest[:ngy], rest[ngy:]) if last else (rest[:1], rest[1:])
        xs = rest[0]
        total = rest[1] if last else outs[0]
        me_x, me_y = lax.axis_index("gx"), lax.axis_index("gy")
        for step in range(ngx):
            xs[rows_at(partner(me_x, step, ngx), block_rows), :] = a_refs[step][...]
        for s in column_tiles(width):
            product = dot(xs[...], w_ref[first : first + depth, s])
            total[:, s] = product if acc is None else acc_ref[:, s] + product
        if last:
            outs[0][...] = total[rows_at(me_y, part), :]
            for step in range(1, ngy):
                outs[step][...] = total[rows_at(target(me_y, step, ngy), part), :].astype(BF16)

    if last:
        out_shape = [pltpu.VMEM((part, width), F32)] + [pltpu.VMEM((part, width), BF16)] * (ngy - 1)
    else:
        out_shape = [pltpu.VMEM((rows, width), F32)]
    extra = [] if acc is None else [acc]
    return pl.pallas_call(
        kernel,
        out_shape=out_shape,
        in_specs=[IN_VMEM] * (ngx + 1 + len(extra)),
        out_specs=[IN_VMEM] * len(out_shape),
        scratch_shapes=[pltpu.VMEM((rows, depth), BF16)]
        + ([pltpu.VMEM((rows, width), F32)] if last else []),
        cost_estimate=cost(2 * rows * depth * width, depth * width * 2),
        compiler_params=pltpu.CompilerParams(vmem_limit_bytes=8 << 20),
        name="project_out",
    )(*blocks, weight, *extra)


def finish(own, received):
    rows, width = own.shape

    def kernel(*refs):
        total = refs[0][...]
        for ref in refs[1:-1]:
            total = total + ref[...].astype(F32)
        refs[-1][...] = total.reshape(rows // 2, 2, width).astype(BF16)

    return pl.pallas_call(
        kernel,
        out_shape=jax.ShapeDtypeStruct((rows // 2, 2, width), BF16),
        in_specs=[IN_VMEM] * (1 + len(received)),
        out_specs=IN_VMEM,
        compiler_params=pltpu.CompilerParams(vmem_limit_bytes=8 << 20),
        name="finish",
    )(own, *received)


def frequencies_of(head_dim):
    half = np.exp(
        np.arange(head_dim // 2, dtype=np.float32)
        * np.float32(-2.0 * math.log(500000.0) / head_dim)
    ).astype(np.float32)
    return jnp.asarray(np.concatenate([half, half])[None])


def on_device(
    ngx, ngy, hidden_in, joined_projection_weight, w_out, key_cache, cached_value_rows, lengths, positions
):
    requests, cache_len, groups, head_dim = key_cache.shape
    keys = key_cache.reshape(requests, cache_len * groups, head_dim)
    values = cached_value_rows.reshape(requests, cache_len * groups, head_dim)
    per_group = joined_projection_weight.shape[1] // (groups * head_dim) - 2
    chunks = chunks_of(groups, per_group)
    ranges = [ranges_of(chunk, per_group, head_dim) for chunk in chunks]
    widths = [sum(width for _, width in r) for r in ranges]

    rows = [hidden_in] + [swap(hidden_in, "gy", s, ngy) for s in range(1, ngy)]
    near, cosine, sine = fetch(
        joined_projection_weight,
        cut(ranges[0], 0, max(head_dim, widths[0] * 4 // 5 // 256 * 256)),
        positions,
        frequencies_of(head_dim),
    )
    joined = []
    for n in range(len(chunks)):
        last = n == len(chunks) - 1
        coming = [] if last else cut(ranges[n + 1], 0, max(head_dim, widths[n + 1] * 3 // 4 // 256 * 256))
        made = project(rows, near, joined_projection_weight, ranges[n], coming, ngx, ngy)
        joined.append((made[0], [swap(made[s], "gx", s, ngx) for s in order_of(ngx)]))
        if not last:
            near = made[ngx]
        if len(rows) > 1:
            rows = [made[-1]]

    attended, pair = [], []
    for n, chunk in enumerate(chunks):
        own, received = joined[n]
        keep = n + 1 < len(chunks) and chunks[n + 1][0][1] > 0
        mine, *pair = attend(
            own, received, pair, keys, values, lengths, cosine, sine, chunk, keep, groups
        )
        attended.append([mine] + [swap(mine, "gx", s, ngx) for s in range(1, ngx)])
    total, first = None, 0
    for n in range(len(chunks)):
        made = project_out(attended[n], total, w_out, first, n == len(chunks) - 1, ngx, ngy)
        first += attended[n][0].shape[1]
        total = made[0]
    return finish(made[0], [swap(made[s], "gy", s, ngy) for s in order_of(ngy)])


def solution(mesh):
    in_specs = (
        P(("groups", "gy"), None, "gx"),
        P("gx", "gy"),
        P("gy", "gx"),
        P(("groups", "gx"), None, "gy", None),
        P(("groups", "gx"), None, "gy", None),
        P(("groups", "gx")),
        P(("groups", "gx")),
    )
    out_specs = P(("groups", "gy"), None, "gx")
    return jax.shard_map(
        functools.partial(on_device, mesh.shape["gx"], mesh.shape["gy"]),
        mesh=mesh,
        in_specs=in_specs,
        out_specs=out_specs,
        check_vma=False,
    )
```
